256 devices in a mesh: inst: 16 (over x_hi, z), px: 2 (over x_lo), pz: 8 (over y, core).
Axes of the slice: x: 4 (x_hi: 2, x_lo: 2; x = x_hi * 2 + x_lo), y: 4, z: 8, core: 2. Of those that a mesh axis runs over, the one named last changes fastest.
Arguments:
- stream_vel: bfloat16 [16, 16, 384, 1024], P('inst', 'px', None, 'pz'), may hold values from -6 to 6
- normal_vel: bfloat16 [16, 16, 384, 1024], P('inst', 'px', None, 'pz'), may hold values from -6 to 6
- span_vel: bfloat16 [16, 16, 384, 1024], P('inst', 'px', None, 'pz'), may hold values from -6 to 6
- adjoint_buoy: float32 [16, 16, 384, 1024], P('inst', 'px', None, 'pz'), may hold values from -6 to 6
- adjoint_normal: float32 [16, 16, 384, 1024], P('inst', 'px', None, 'pz'), may hold values from -6 to 6
Outputs:
- pseudo_update: float32 [16, 16, 384, 1024], P('inst', 'px', None, 'pz')
The draws below stay inside these ranges and needn't reach their ends.
All inputs are finite; a program needn't handle non-finite values.
Results may differ from the reference program's by a relative error of at most 0.0003.
Values sent between devices are 32-bit elements; how exact they have to be, the bound alone decides.
No kernel may reach another device: no remote copies, remote signals or barrier semaphores. Data moves between devices by JAX's collectives and lax.ppermute only.
A program may use at most 128 MiB of HBM per device.

```python
import math
import jax
import jax.numpy as jnp
from jax import lax

NX = 1024
NY = 384
NZ = 16
NT = 16


def shard_levels(key, shape, cuts, smallest, high):
    level, own = 1.0, jax.random.fold_in(key, 6)
    for position, shards_of in cuts:
        heights = jnp.exp(jax.random.uniform(jax.random.fold_in(own, position), (shards_of,), jnp.float32, smallest / len(cuts), high / len(cuts)))
        level = level * jnp.repeat(heights, shape[position] // shards_of).reshape([-1 if axis == position else 1 for axis in range(len(shape))])
    return level


def bell_draw(rng, shape, scale, bound, shards=(), dtype=jnp.bfloat16):
    level = shard_levels(rng, shape, shards, -0.22, 0.18) if shards else 1.0
    entries = jax.random.normal(rng, shape, jnp.float32) * scale * level
    return jnp.minimum(jnp.maximum(entries, -bound), bound).astype(dtype)


def setup_inputs(seed: int = 0) -> dict:
    splits = jax.random.split(jax.random.key(seed), 6)
    return {
        "stream_vel": bell_draw(splits[0], (NT, NZ, NY, NX), 1.0, 6.0, ((0, 16), (1, 2), (3, 8))),
        "normal_vel": bell_draw(splits[1], (NT, NZ, NY, NX), 1.0, 6.0, ((0, 16), (1, 2), (3, 8))),
        "span_vel": bell_draw(splits[2], (NT, NZ, NY, NX), 1.0, 6.0, ((0, 16), (1, 2), (3, 8))),
        "adjoint_buoy": bell_draw(splits[3], (NT, NZ, NY, NX), 1.0, 6.0, ((0, 16), (1, 2), (3, 8)), jnp.float32),
        "adjoint_normal": bell_draw(splits[4], (NT, NZ, NY, NX), 1.0, 6.0, ((0, 16), (1, 2), (3, 8)), jnp.float32),
    }


box_length = 4.0 * math.pi
diffusivity = 1e-2
omega_tide = 4.0
coupling = 50.0
span_step = 0.05


def fourier_first(count):
    points = jnp.arange(count)
    differ = points[:, None] - points[None, :]
    parity = 1.0 - 2.0 * (differ % 2).astype(jnp.float32)
    tangent = jnp.tan(jnp.pi * differ.astype(jnp.float32) / count)
    safe_tan = jnp.where(differ == 0, 1.0, tangent)
    return jnp.where(differ == 0, 0.0, 0.5 * parity / safe_tan).astype(jnp.float32)


def fourier_second(count):
    points = jnp.arange(count)
    differ = points[:, None] - points[None, :]
    parity = 1.0 - 2.0 * (differ % 2).astype(jnp.float32)
    sine = jnp.sin(jnp.pi * differ.astype(jnp.float32) / count)
    safe_sine = jnp.where(differ == 0, 1.0, sine)
    centre = -(count * count) / 12.0 - 1.0 / 6.0
    return jnp.where(differ == 0, centre, -0.5 * parity / (safe_sine * safe_sine)).astype(jnp.float32)


def wall_table(count):
    order = count - 1
    points = jnp.arange(count)
    angles = jnp.pi * points.astype(jnp.float32) / order
    coords = jnp.cos(angles)
    ends = (points == 0) | (points == order)
    scaled = jnp.where(ends, 2.0, 1.0) * (1.0 - 2.0 * (points % 2).astype(jnp.float32))
    total = (points[:, None] + points[None, :]).astype(jnp.float32)
    differ = points[:, None] - points[None, :]
    gap = -2.0 * jnp.sin(jnp.pi * total / (2 * order)) * jnp.sin(jnp.pi * differ.astype(jnp.float32) / (2 * order))
    safe_gap = jnp.where(differ == 0, 1.0, gap)
    offdiag = scaled[:, None] / scaled[None, :] / safe_gap
    sine_sq = jnp.where(ends, 1.0, jnp.sin(angles) ** 2)
    corner = (2.0 * order * order + 1.0) / 6.0
    centre = jnp.where(points == 0, corner, jnp.where(points == order, -corner, -coords / (2.0 * sine_sq)))
    table = jnp.where(differ == 0, jnp.diag(centre), offdiag)
    spacing = (jnp.pi / order) * (jnp.sin(angles) + jnp.pi / order)
    return table.astype(jnp.float32), spacing.astype(jnp.float32)


def reference(stream_vel, normal_vel, span_vel, adjoint_buoy, adjoint_normal):
    high = lax.Precision.HIGHEST
    wave = 2.0 * math.pi / box_length
    grad_table = wave * fourier_first(NX)
    curv_table = wave * wave * fourier_second(NX)
    normal_table, spacing = wall_table(NY)
    instant_table = omega_tide * fourier_first(NT)
    grid_step = box_length / NX
    time_term = jnp.einsum('ji,jzyx->izyx', instant_table, adjoint_buoy, precision=high)

    def one_instance(inputs):
        stream, normal, span, buoy, adjn, timed = inputs
        stream = stream.astype(jnp.float32)
        normal = normal.astype(jnp.float32)
        span = span.astype(jnp.float32)
        grad_x = jnp.einsum('zyk,ik->zyi', buoy, grad_table, precision=high)
        curv_x = jnp.einsum('zyk,ik->zyi', buoy, curv_table, precision=high)
        grad_y = jnp.einsum('jk,zkx->zjx', normal_table, buoy, precision=high)
        curv_y = jnp.einsum('jk,zkx->zjx', normal_table, grad_y, precision=high)
        above_plane = jnp.roll(buoy, -1, 0)
        below_plane = jnp.roll(buoy, 1, 0)
        grad_z = (above_plane - below_plane) / (2.0 * span_step)
        curv_z = (above_plane - 2.0 * buoy + below_plane) / (span_step * span_step)
        advect = stream * grad_x + normal * grad_y + span * grad_z
        diffuse = curv_x + curv_y + curv_z
        residual = -timed - advect - diffusivity * diffuse - coupling * adjn
        inv_sq = 1.0 / (spacing * spacing)
        radius = (omega_tide * NT / 2.0 + jnp.abs(stream) / grid_step
                  + jnp.abs(normal) / spacing[:, None] + jnp.abs(span) / span_step
                  + 2.0 * diffusivity * (1.0 / (grid_step * grid_step) + inv_sq[:, None] + 1.0 / (span_step * span_step)))
        return residual / (1.0 + radius)

    return lax.map(one_instance, (stream_vel, normal_vel, span_vel, adjoint_buoy, adjoint_normal, time_term))
```

```python
import functools
import math

import jax
import jax.numpy as jnp
import ml_dtypes
import numpy as np
from jax import lax
from jax.experimental import pallas as pl
from jax.experimental.pallas import tpu as pltpu
from jax.sharding import PartitionSpec as P

box_length = 4.0 * math.pi
diffusivity = 0.01
omega_tide = 4.0
coupling = 50.0
span_step = 0.05

f32 = jnp.float32
bf16 = jnp.bfloat16


def first_line(count):
    d = np.arange(count)
    sign = 1.0 - 2.0 * (d % 2)
    safe = np.where(d == 0, 1.0, np.tan(np.pi * d / count))
    return np.where(d == 0, 0.0, 0.5 * sign / safe)


def second_line(count):
    d = np.arange(count)
    sign = 1.0 - 2.0 * (d % 2)
    safe = np.where(d == 0, 1.0, np.sin(np.pi * d / count))
    return np.where(d == 0, -(count * count) / 12.0 - 1.0 / 6.0, -0.5 * sign / (safe * safe))


def wall_table(count):
    order = count - 1
    j = np.arange(count)
    angle = np.pi * j / order
    ends = (j == 0) | (j == order)
    c = np.where(ends, 2.0, 1.0) * (1.0 - 2.0 * (j % 2))
    total = j[:, None] + j[None, :]
    differ = j[:, None] - j[None, :]
    gap = -2.0 * np.sin(np.pi * total / (2 * order)) * np.sin(np.pi * differ / (2 * order))
    table = c[:, None] / c[None, :] / np.where(differ == 0, 1.0, gap)
    corner = (2.0 * order * order + 1.0) / 6.0
    sine_sq = np.where(ends, 1.0, np.sin(angle) ** 2)
    centre = -np.cos(angle) / (2.0 * sine_sq)
    centre[0], centre[order] = corner, -corner
    table = np.where(differ == 0, np.diag(centre), table)
    spacing = np.pi / order * (np.sin(angle) + np.pi / order)
    return table, spacing


def three_parts(table, axis):
    high = table.astype(np.float32).astype(ml_dtypes.bfloat16)
    low = (table - high.astype(np.float64)).astype(np.float32).astype(ml_dtypes.bfloat16)
    return np.concatenate([high, high, low], axis=axis)


def split(x):
    high = x.astype(bf16)
    return high, (x - high.astype(f32)).astype(bf16)


def derivatives(blocks, table):
    planes, rows, width = blocks[0].shape
    parts = [split(x.reshape(planes * rows, width)) for x in blocks]
    high, low = ([p[i] for p in parts] for i in range(2))
    both = jnp.dot(jnp.concatenate(high + low + high, axis=1), table, preferred_element_type=f32)
    return both[:, :width].reshape(planes, rows, width), both[:, width:].reshape(planes, rows, width)


def wall_kernel(dx, core_ref, wall_ref, line_ref, scale_ref, b_ref, edge_ref, other_ref, u_ref, v_ref, w_ref, n_ref, part_ref, inv_ref, token_ref):
    count, rows, width = b_ref.shape
    pair = u_ref.shape[0]
    start = pl.program_id(0) * pair
    here = b_ref[pl.ds(start, pair)]
    high, low = split(jnp.concatenate([here[i] for i in range(pair)], axis=1))
    both = jnp.dot(wall_ref[...], jnp.concatenate([high, low, high], axis=0), preferred_element_type=f32)
    grad_x, curv_x = derivatives([here, other_ref[...]], line_ref[0])
    for i in range(pair):
        z = start + i
        lanes = slice(i * width, (i + 1) * width)
        u, v, w = (r[i].astype(f32) for r in (u_ref, v_ref, w_ref))
        above = jnp.where(z == count - 1, edge_ref[0], b_ref[jnp.minimum(z + 1, count - 1)])
        below = jnp.where(z == 0, edge_ref[1], b_ref[jnp.maximum(z - 1, 0)])
        grad_z = (above - below) * (1.0 / (2.0 * span_step))
        curv_z = (above - 2.0 * here[i] + below) * (diffusivity / (span_step * span_step))
        radius = scale_ref[1] + jnp.abs(u) * (1.0 / dx) + jnp.abs(v) * scale_ref[0] + jnp.abs(w) * (1.0 / span_step)
        inv_ref[i] = 1.0 / radius
        advect = u * grad_x[i] + v * both[:rows, lanes] + w * grad_z
        part_ref[i] = -advect - (curv_x[i] + both[rows:, lanes] + curv_z) - coupling * n_ref[i]
    token_ref[...] = jnp.zeros_like(token_ref)


def early_kernel(core_ref, table_ref, *refs):
    blocks, (u_ref, part_ref, out_ref, token_ref) = refs[:4], refs[4:]
    grad_x, curv_x = derivatives([r[...] for r in blocks], table_ref[0])
    out_ref[...] = part_ref[...] - (u_ref[...].astype(f32) * grad_x + curv_x)
    token_ref[...] = jnp.zeros_like(token_ref)


def late_kernel(half, core_ref, table_ref, *refs):
    lower, upper = refs[:2], refs[2:4]
    u_ref, steps_ref, out_ref, token_ref = refs[4:]
    second = pl.program_id(0) >= half
    grad_x, curv_x = derivatives([jnp.where(second, y[...], x[...]) for x, y in zip(lower, upper)], table_ref[0])
    out_ref[...] = steps_ref[...] - (u_ref[...].astype(f32) * grad_x + curv_x)
    token_ref[...] = jnp.zeros_like(token_ref)


def halves_kernel(before_ref, after_ref, onward_ref, return_ref, sems):
    half = onward_ref.shape[0]
    copies = [pltpu.make_async_copy(before_ref.at[k], onward_ref.at[k], sems.at[0, k]) for k in range(half)]
    copies += [pltpu.make_async_copy(after_ref.at[half + k], return_ref.at[k], sems.at[1, k]) for k in range(half)]
    for copy in copies:
        copy.start()
    for copy in copies:
        copy.wait()


def follow_kernel(*refs):
    pass


def in_parts(count, sources, buffers, result, target, in_sems, out_sems, work):
    def part(k):
        return [pltpu.make_async_copy(x.at[at], y.at[at], in_sems.at[i, k]) for i, (x, y) in enumerate(zip(sources, buffers))]

    def out(k):
        return pltpu.make_async_copy(result.at[at], target.at[at], out_sems.at[k])

    for k in range(count):
        at = work.where(k)
        for copy in part(k):
            copy.start()
    for k in range(count):
        at = work.where(k)
        for copy in part(k):
            copy.wait()
        work.do(k)
        out(k).start()
    for k in range(count):
        at = work.where(k)
        out(k).wait()


class TimePart:
    def __init__(self, weights, size, source, result):
        self.weights, self.size, self.source, self.result = weights, size, source, result

    def where(self, k):
        return (slice(None), pl.ds(k * self.size, self.size))

    def do(self, k):
        weights, count = self.weights, self.source.shape[0]
        half = count // 2

        def body(step, carry):
            rows = pl.ds(pl.multiple_of(k * self.size + step * 8, 8), 8)
            b = [self.source[i, rows, :] for i in range(count)]
            totals = [weights[half] * b[(i + half) % count] for i in range(count)]
            for i in range(half):
                for d in range(1, half):
                    differ = b[(i + d) % count] - b[(i - d) % count]
                    totals[i] = totals[i] + weights[d] * differ
                    totals[i + half] = totals[i + half] - weights[half - d] * differ
            for i in range(count):
                self.result[i, rows, :] = totals[i]
            return carry

        lax.fori_loop(0, self.size // 8, body, 0)


class LastPart:
    def __init__(self, size, steps, time, inv, result):
        self.size, self.steps, self.time, self.inv, self.result = size, steps, time, inv, result

    def where(self, k):
        return (pl.ds(k * self.size, self.size),)

    def do(self, k):
        at = self.where(k)
        self.result[at] = (self.steps[at] - self.time[at]) * self.inv[at]


def time_kernel(weights, parts, in_ref, *refs):
    out_ref, source, result, in_sems, out_sems = refs[-5:]
    work = TimePart(weights, in_ref.shape[1] // parts, source, result)
    in_parts(parts, [in_ref], [source], result, out_ref, in_sems, out_sems, work)


def last_kernel(parts, time_ref, inv_ref, steps_ref, out_ref, steps, result, in_sems, out_sems):
    work = LastPart(steps_ref.shape[0] // parts, steps, time_ref, inv_ref, result)
    in_parts(parts, [steps_ref], [steps], result, out_ref, in_sems, out_sems, work)


def on_device(stream_vel, normal_vel, span_vel, adjoint_buoy, adjoint_normal):
    _, planes, rows, width = adjoint_buoy.shape
    count_x, count_i, count_p = (lax.axis_size(a) for a in ("pz", "inst", "px"))
    full = width * count_x
    dx = box_length / full
    wave = 2.0 * math.pi / box_length

    cores = 2
    groups = (0,), (-1, 1), (2,)

    def line_table(core, chips):
        offsets = [cores * step + other - core for step in chips for other in (core, 1 - core)]
        k = np.concatenate([np.arange(width) + width * o for o in offsets])
        d = (np.arange(width)[None, :] - k[:, None]) % full
        table = np.concatenate([wave * first_line(full)[d], diffusivity * wave * wave * second_line(full)[d]], axis=1)
        return three_parts(table, 0)

    first, early, late = (jnp.asarray(np.stack([line_table(c, t) for c in range(cores)])) for t in groups)
    normal_table, spacing = wall_table(rows)
    wall = np.concatenate([normal_table, diffusivity * (normal_table @ normal_table)], axis=0)
    wall = jnp.asarray(three_parts(wall, 1))
    steady = 1.0 + omega_tide * count_i / 2.0 + 2.0 * diffusivity * (1.0 / dx**2 + 1.0 / spacing**2 + 1.0 / span_step**2)
    scale = np.stack([1.0 / spacing, steady]).astype(np.float32)[:, :, None]
    scale = np.broadcast_to(scale, (2, rows, width))
    weights = [float(x) for x in omega_tide * first_line(count_i)]

    core = (lax.axis_index("pz") % cores).astype(jnp.int32).reshape(1)

    b, u, v, w, n = (x[0] for x in (adjoint_buoy, stream_vel, normal_vel, span_vel, adjoint_normal))

    share = planes * rows // count_i
    exchange = functools.partial(lax.all_to_all, axis_name="inst", split_axis=0, concat_axis=0, tiled=True)
    sent = exchange(b.reshape(count_i, share, width))

    members = range(count_x)
    onward = [(i, (i + cores) % count_x) for i in members]
    return_ = [(j, i) for i, j in onward]
    partner = [(i, i ^ 1) for i in members]
    half = planes // 2
    before = lax.ppermute(b, "pz", onward)
    after = lax.ppermute(b, "pz", return_)
    other = lax.ppermute(b, "pz", partner)
    swap = [(i, (i + 1) % count_p) for i in range(count_p)]
    back = [(j, i) for i, j in swap]
    if count_p == 2:
        edge = lax.ppermute(jnp.stack([b[0], b[planes - 1]]), "px", swap)
    else:
        edge = jnp.stack([lax.ppermute(b[0], "px", back), lax.ppermute(b[planes - 1], "px", swap)])

    pair = 2
    anywhere, in_memory = pl.BlockSpec(memory_space=pl.ANY), pl.BlockSpec(memory_space=pltpu.HBM)
    params = lambda size: pltpu.CompilerParams(vmem_limit_bytes=size * 2**20)
    spec = lambda f: pl.BlockSpec((pair, rows, width), lambda s, c: (f(s), 0, 0))
    two = spec(lambda s: s)
    fixed = lambda *shape: pl.BlockSpec(shape, lambda s, c: (0,) * len(shape))
    table = lambda t: pl.BlockSpec((1,) + t.shape[1:], lambda s, c: (c[0], 0, 0))
    part, inv, token = pl.pallas_call(
        functools.partial(wall_kernel, dx),
        out_shape=[jax.ShapeDtypeStruct(b.shape, f32)] * 2 + [jax.ShapeDtypeStruct((8, width), f32)],
        grid_spec=pltpu.PrefetchScalarGridSpec(
            num_scalar_prefetch=1,
            grid=(planes // pair,),
            in_specs=[fixed(*wall.shape), table(first), fixed(*scale.shape), fixed(*b.shape), fixed(2, rows, width)] + [two] * 5,
            out_specs=[two] * 2 + [fixed(8, width)],
        ),
        compiler_params=params(24),
        cost_estimate=pl.CostEstimate(flops=16 * rows * b.size, bytes_accessed=b.size * 28, transcendentals=0),
        name="wall_terms",
    )(core, wall, first, jnp.asarray(scale), b, edge, other, u, v, w, n)

    def follow(name, *arrays, after):
        return pl.pallas_call(
            follow_kernel,
            out_shape=[jax.ShapeDtypeStruct(x.shape, f32) for x in arrays],
            in_specs=[anywhere] * (len(arrays) + 1),
            out_specs=[anywhere] * len(arrays),
            input_output_aliases={i: i for i in range(len(arrays))},
            compiler_params=params(1),
            name=name,
        )(*arrays, after)

    onward_half, return_half = pl.pallas_call(
        halves_kernel,
        out_shape=[jax.ShapeDtypeStruct((half, rows, width), f32)] * 2,
        in_specs=[anywhere] * 2,
        out_specs=[anywhere] * 2,
        scratch_shapes=[pltpu.SemaphoreType.DMA((2, half))],
        compiler_params=params(1),
        cost_estimate=pl.CostEstimate(flops=0, bytes_accessed=b.size * 8, transcendentals=0),
        name="halves",
    )(before, after)
    far_0 = lax.ppermute(onward_half, "pz", onward)
    far_1 = lax.ppermute(return_half, "pz", return_)

    parts = 4
    applied = pl.pallas_call(
        functools.partial(time_kernel, weights, parts),
        out_shape=jax.ShapeDtypeStruct(sent.shape, f32),
        in_specs=[in_memory, anywhere],
        out_specs=in_memory,
        scratch_shapes=[pltpu.VMEM(sent.shape, f32)] * 2
        + [pltpu.SemaphoreType.DMA((1, parts)), pltpu.SemaphoreType.DMA((parts,))],
        compiler_params=params(60),
        cost_estimate=pl.CostEstimate(flops=sent.size * 16, bytes_accessed=sent.size * 8, transcendentals=0),
        name="time_term",
    )(sent, token)
    time_term = exchange(applied).reshape(planes, rows, width)

    with_other = lambda r: (r, lax.ppermute(r, "pz", partner))
    last_low = half // pair - 1
    in_lower, in_upper = spec(lambda s: jnp.minimum(s, last_low)), spec(lambda s: jnp.maximum(s - last_low - 1, 0))

    def line_terms(kernel, name, chips, size, specs, operands):
        return pl.pallas_call(
            kernel,
            out_shape=[jax.ShapeDtypeStruct(b.shape, f32), jax.ShapeDtypeStruct((8, width), f32)],
            grid_spec=pltpu.PrefetchScalarGridSpec(
                num_scalar_prefetch=1, grid=(planes // pair,), in_specs=specs, out_specs=[two, fixed(8, width)]
            ),
            compiler_params=params(size),
            cost_estimate=pl.CostEstimate(
                flops=12 * chips * cores * width * b.size, bytes_accessed=b.size * 4 * (3 + 2 * chips), transcendentals=0
            ),
            name=name,
        )(core, *operands)

    operands = (early, *with_other(before), *with_other(after), u, part)
    steps, token = line_terms(early_kernel, "early_terms", 2, 60, [table(early)] + [two] * 6, operands)
    far_0, far_1 = follow("follow_early", far_0, far_1, after=token)
    operands = (late, *with_other(far_0), *with_other(far_1), u, steps)
    specs = [table(late)] + [in_lower] * 2 + [in_upper] * 2 + [two] * 2
    steps, _ = line_terms(functools.partial(late_kernel, half // pair), "late_terms", 1, 60, specs, operands)

    out = pl.pallas_call(
        functools.partial(last_kernel, planes),
        out_shape=jax.ShapeDtypeStruct(b.shape, f32),
        in_specs=[pl.BlockSpec(memory_space=pltpu.VMEM)] * 2 + [in_memory],
        out_specs=in_memory,
        scratch_shapes=[pltpu.VMEM(b.shape, f32)] * 2
        + [pltpu.SemaphoreType.DMA((1, planes)), pltpu.SemaphoreType.DMA((planes,))],
        compiler_params=params(58),
        cost_estimate=pl.CostEstimate(flops=2 * b.size, bytes_accessed=b.size * 16, transcendentals=0),
        name="last",
    )(time_term, inv, steps)
    return out[None]


def solution(mesh):
    spec = P("inst", "px", None, "pz")
    return jax.shard_map(on_device, mesh=mesh, in_specs=(spec,) * 5, out_specs=spec, check_vma=False)
```

```python
import functools
import math

import jax
import jax.numpy as jnp
import ml_dtypes
import numpy as np
from jax import lax
from jax.experimental import pallas as pl
from jax.experimental.pallas import tpu as pltpu
from jax.sharding import PartitionSpec as P

box_length = 4.0 * math.pi
diffusivity = 0.01
omega_tide = 4.0
coupling = 50.0
span_step = 0.05

f32 = jnp.float32
bf16 = jnp.bfloat16


def first_line(count):
    d = np.arange(count)
    sign = 1.0 - 2.0 * (d % 2)
    safe = np.where(d == 0, 1.0, np.tan(np.pi * d / count))
    return np.where(d == 0, 0.0, 0.5 * sign / safe)


def second_line(count):
    d = np.arange(count)
    sign = 1.0 - 2.0 * (d % 2)
    safe = np.where(d == 0, 1.0, np.sin(np.pi * d / count))
    return np.where(d == 0, -(count * count) / 12.0 - 1.0 / 6.0, -0.5 * sign / (safe * safe))


def wall_table(count):
    order = count - 1
    j = np.arange(count)
    angle = np.pi * j / order
    ends = (j == 0) | (j == order)
    c = np.where(ends, 2.0, 1.0) * (1.0 - 2.0 * (j % 2))
    total = j[:, None] + j[None, :]
    differ = j[:, None] - j[None, :]
    gap = -2.0 * np.sin(np.pi * total / (2 * order)) * np.sin(np.pi * differ / (2 * order))
    table = c[:, None] / c[None, :] / np.where(differ == 0, 1.0, gap)
    corner = (2.0 * order * order + 1.0) / 6.0
    sine_sq = np.where(ends, 1.0, np.sin(angle) ** 2)
    centre = -np.cos(angle) / (2.0 * sine_sq)
    centre[0], centre[order] = corner, -corner
    table = np.where(differ == 0, np.diag(centre), table)
    spacing = np.pi / order * (np.sin(angle) + np.pi / order)
    return table, spacing


def three_parts(table, axis):
    high = table.astype(np.float32).astype(ml_dtypes.bfloat16)
    low = (table - high.astype(np.float64)).astype(np.float32).astype(ml_dtypes.bfloat16)
    return np.concatenate([high, high, low], axis=axis)


def split(x):
    high = x.astype(bf16)
    return high, (x - high.astype(f32)).astype(bf16)


def derivatives(blocks, table):
    planes, rows, width = blocks[0].shape
    parts = [split(x.reshape(planes * rows, width)) for x in blocks]
    high, low = ([p[i] for p in parts] for i in range(2))
    both = jnp.dot(jnp.concatenate(high + low + high, axis=1), table, preferred_element_type=f32)
    return both[:, :width].reshape(planes, rows, width), both[:, width:].reshape(planes, rows, width)


def wall_kernel(dx, core_ref, wall_ref, line_ref, scale_ref, b_ref, edge_ref, other_ref, u_ref, v_ref, w_ref, n_ref, part_ref, inv_ref, token_ref):
    count, rows, width = b_ref.shape
    pair = u_ref.shape[0]
    start = pl.program_id(0) * pair
    here = b_ref[pl.ds(start, pair)]
    high, low = split(jnp.concatenate([here[i] for i in range(pair)], axis=1))
    both = jnp.dot(wall_ref[...], jnp.concatenate([high, low, high], axis=0), preferred_element_type=f32)
    grad_x, curv_x = derivatives([here, other_ref[...]], line_ref[0])
    for i in range(pair):
        z = start + i
        lanes = slice(i * width, (i + 1) * width)
        u, v, w = (r[i].astype(f32) for r in (u_ref, v_ref, w_ref))
        above = jnp.where(z == count - 1, edge_ref[0], b_ref[jnp.minimum(z + 1, count - 1)])
        below = jnp.where(z == 0, edge_ref[1], b_ref[jnp.maximum(z - 1, 0)])
        grad_z = (above - below) * (1.0 / (2.0 * span_step))
        curv_z = (above - 2.0 * here[i] + below) * (diffusivity / (span_step * span_step))
        radius = scale_ref[1] + jnp.abs(u) * (1.0 / dx) + jnp.abs(v) * scale_ref[0] + jnp.abs(w) * (1.0 / span_step)
        inv_ref[i] = 1.0 / radius
        advect = u * grad_x[i] + v * both[:rows, lanes] + w * grad_z
        part_ref[i] = -advect - (curv_x[i] + both[rows:, lanes] + curv_z) - coupling * n_ref[i]
    token_ref[...] = jnp.zeros_like(token_ref)


def early_kernel(core_ref, table_ref, *refs):
    blocks, (u_ref, part_ref, out_ref, token_ref) = refs[:4], refs[4:]
    grad_x, curv_x = derivatives([r[...] for r in blocks], table_ref[0])
    out_ref[...] = part_ref[...] - (u_ref[...].astype(f32) * grad_x + curv_x)
    token_ref[...] = jnp.zeros_like(token_ref)


def late_kernel(half, core_ref, table_ref, *refs):
    lower, upper = refs[:2], refs[2:4]
    u_ref, steps_ref, out_ref, token_ref = refs[4:]
    second = pl.program_id(0) >= half
    grad_x, curv_x = derivatives([jnp.where(second, y[...], x[...]) for x, y in zip(lower, upper)], table_ref[0])
    out_ref[...] = steps_ref[...] - (u_ref[...].astype(f32) * grad_x + curv_x)
    token_ref[...] = jnp.zeros_like(token_ref)


def halves_kernel(before_ref, after_ref, onward_ref, return_ref, held, in_sems, out_sems):
    half = onward_ref.shape[0]
    planes = [(before_ref.at[k], onward_ref.at[k]) for k in range(half)]
    planes += [(after_ref.at[half + k], return_ref.at[k]) for k in range(half)]
    come = [pltpu.make_async_copy(x, held.at[k], in_sems.at[k]) for k, (x, _) in enumerate(planes)]
    go = [pltpu.make_async_copy(held.at[k], y, out_sems.at[k]) for k, (_, y) in enumerate(planes)]
    for copy in come:
        copy.start()
    for first, second in zip(come, go):
        first.wait()
        second.start()
    for copy in go:
        copy.wait()


def follow_kernel(*refs):
    pass


def in_parts(count, sources, buffers, result, target, in_sems, out_sems, work):
    def part(k):
        return [pltpu.make_async_copy(x.at[at], y.at[at], in_sems.at[i, k]) for i, (x, y) in enumerate(zip(sources, buffers))]

    def out(k):
        return pltpu.make_async_copy(result.at[at], target.at[at], out_sems.at[k])

    for k in range(count):
        at = work.where(k)
        for copy in part(k):
            copy.start()
    for k in range(count):
        at = work.where(k)
        for copy in part(k):
            copy.wait()
        work.do(k)
        out(k).start()
    for k in range(count):
        at = work.where(k)
        out(k).wait()


class TimePart:
    def __init__(self, weights, size, source, result):
        self.weights, self.size, self.source, self.result = weights, size, source, result

    def where(self, k):
        return (slice(None), pl.ds(k * self.size, self.size))

    def do(self, k):
        weights, count = self.weights, self.source.shape[0]
        half = count // 2

        def body(step, carry):
            rows = pl.ds(pl.multiple_of(k * self.size + step * 8, 8), 8)
            b = [self.source[i, rows, :] for i in range(count)]
            totals = [weights[half] * b[(i + half) % count] for i in range(count)]
            for i in range(half):
                for d in range(1, half):
                    differ = b[(i + d) % count] - b[(i - d) % count]
                    totals[i] = totals[i] + weights[d] * differ
                    totals[i + half] = totals[i + half] - weights[half - d] * differ
            for i in range(count):
                self.result[i, rows, :] = totals[i]
            return carry

        lax.fori_loop(0, self.size // 8, body, 0)


class LastPart:
    def __init__(self, size, steps, time, inv, result):
        self.size, self.steps, self.time, self.inv, self.result = size, steps, time, inv, result

    def where(self, k):
        return (pl.ds(k * self.size, self.size),)

    def do(self, k):
        at = self.where(k)
        self.result[at] = (self.steps[at] - self.time[at]) * self.inv[at]


def time_kernel(weights, parts, in_ref, *refs):
    out_ref, source, result, in_sems, out_sems = refs[-5:]
    work = TimePart(weights, in_ref.shape[1] // parts, source, result)
    in_parts(parts, [in_ref], [source], result, out_ref, in_sems, out_sems, work)


def last_kernel(parts, time_ref, inv_ref, steps_ref, out_ref, result, in_sems, out_sems):
    work = LastPart(steps_ref.shape[0] // parts, steps_ref, time_ref, inv_ref, result)
    in_parts(parts, [], [], result, out_ref, in_sems, out_sems, work)


def on_device(stream_vel, normal_vel, span_vel, adjoint_buoy, adjoint_normal):
    _, planes, rows, width = adjoint_buoy.shape
    count_x, count_i, count_p = (lax.axis_size(a) for a in ("pz", "inst", "px"))
    full = width * count_x
    dx = box_length / full
    wave = 2.0 * math.pi / box_length

    cores = 2
    groups = (0,), (-1, 1), (2,)

    def line_table(core, chips):
        offsets = [cores * step + other - core for step in chips for other in (core, 1 - core)]
        k = np.concatenate([np.arange(width) + width * o for o in offsets])
        d = (np.arange(width)[None, :] - k[:, None]) % full
        table = np.concatenate([wave * first_line(full)[d], diffusivity * wave * wave * second_line(full)[d]], axis=1)
        return three_parts(table, 0)

    first, early, late = (jnp.asarray(np.stack([line_table(c, t) for c in range(cores)])) for t in groups)
    normal_table, spacing = wall_table(rows)
    wall = np.concatenate([normal_table, diffusivity * (normal_table @ normal_table)], axis=0)
    wall = jnp.asarray(three_parts(wall, 1))
    steady = 1.0 + omega_tide * count_i / 2.0 + 2.0 * diffusivity * (1.0 / dx**2 + 1.0 / spacing**2 + 1.0 / span_step**2)
    scale = np.stack([1.0 / spacing, steady]).astype(np.float32)[:, :, None]
    scale = np.broadcast_to(scale, (2, rows, width))
    weights = [float(x) for x in omega_tide * first_line(count_i)]

    core = (lax.axis_index("pz") % cores).astype(jnp.int32).reshape(1)

    b, u, v, w, n = (x[0] for x in (adjoint_buoy, stream_vel, normal_vel, span_vel, adjoint_normal))

    share = planes * rows // count_i
    exchange = functools.partial(lax.all_to_all, axis_name="inst", split_axis=0, concat_axis=0, tiled=True)
    sent = exchange(b.reshape(count_i, share, width))

    members = range(count_x)
    onward = [(i, (i + cores) % count_x) for i in members]
    return_ = [(j, i) for i, j in onward]
    partner = [(i, i ^ 1) for i in members]
    half = planes // 2
    before = lax.ppermute(b, "pz", onward)
    after = lax.ppermute(b, "pz", return_)
    other = lax.ppermute(b, "pz", partner)
    swap = [(i, (i + 1) % count_p) for i in range(count_p)]
    back = [(j, i) for i, j in swap]
    if count_p == 2:
        edge = lax.ppermute(jnp.stack([b[0], b[planes - 1]]), "px", swap)
    else:
        edge = jnp.stack([lax.ppermute(b[0], "px", back), lax.ppermute(b[planes - 1], "px", swap)])

    pair = 2
    anywhere, in_memory = pl.BlockSpec(memory_space=pl.ANY), pl.BlockSpec(memory_space=pltpu.HBM)
    params = lambda size: pltpu.CompilerParams(vmem_limit_bytes=size * 2**20)
    spec = lambda f: pl.BlockSpec((pair, rows, width), lambda s, c: (f(s), 0, 0))
    two = spec(lambda s: s)
    fixed = lambda *shape: pl.BlockSpec(shape, lambda s, c: (0,) * len(shape))
    table = lambda t: pl.BlockSpec((1,) + t.shape[1:], lambda s, c: (c[0], 0, 0))
    part, inv, token = pl.pallas_call(
        functools.partial(wall_kernel, dx),
        out_shape=[jax.ShapeDtypeStruct(b.shape, f32)] * 2 + [jax.ShapeDtypeStruct((8, width), f32)],
        grid_spec=pltpu.PrefetchScalarGridSpec(
            num_scalar_prefetch=1,
            grid=(planes // pair,),
            in_specs=[fixed(*wall.shape), table(first), fixed(*scale.shape), fixed(*b.shape), fixed(2, rows, width)] + [two] * 5,
            out_specs=[two] * 2 + [fixed(8, width)],
        ),
        compiler_params=params(24),
        cost_estimate=pl.CostEstimate(flops=16 * rows * b.size, bytes_accessed=b.size * 28, transcendentals=0),
        name="wall_terms",
    )(core, wall, first, jnp.asarray(scale), b, edge, other, u, v, w, n)

    def follow(name, *arrays, after):
        return pl.pallas_call(
            follow_kernel,
            out_shape=[jax.ShapeDtypeStruct(x.shape, f32) for x in arrays],
            in_specs=[anywhere] * (len(arrays) + 1),
            out_specs=[anywhere] * len(arrays),
            input_output_aliases={i: i for i in range(len(arrays))},
            compiler_params=params(1),
            name=name,
        )(*arrays, after)

    onward_half, return_half = pl.pallas_call(
        halves_kernel,
        out_shape=[jax.ShapeDtypeStruct((half, rows, width), f32)] * 2,
        in_specs=[anywhere] * 2,
        out_specs=[anywhere] * 2,
        scratch_shapes=[pltpu.VMEM(b.shape, f32)] + [pltpu.SemaphoreType.DMA((2 * half,))] * 2,
        compiler_params=params(8),
        cost_estimate=pl.CostEstimate(flops=0, bytes_accessed=b.size * 8, transcendentals=0),
        name="halves",
    )(before, after)
    far_0 = lax.ppermute(onward_half, "pz", onward)
    far_1 = lax.ppermute(return_half, "pz", return_)

    parts = 8
    applied = pl.pallas_call(
        functools.partial(time_kernel, weights, parts),
        out_shape=jax.ShapeDtypeStruct(sent.shape, f32),
        in_specs=[in_memory, anywhere],
        out_specs=in_memory,
        scratch_shapes=[pltpu.VMEM(sent.shape, f32)] * 2
        + [pltpu.SemaphoreType.DMA((1, parts)), pltpu.SemaphoreType.DMA((parts,))],
        compiler_params=params(60),
        cost_estimate=pl.CostEstimate(flops=sent.size * 16, bytes_accessed=sent.size * 8, transcendentals=0),
        name="time_term",
    )(sent, token)
    time_term = exchange(applied).reshape(planes, rows, width)

    with_other = lambda r: (r, lax.ppermute(r, "pz", partner))
    last_low = half // pair - 1
    in_lower, in_upper = spec(lambda s: jnp.minimum(s, last_low)), spec(lambda s: jnp.maximum(s - last_low - 1, 0))

    def line_terms(kernel, name, chips, size, specs, operands):
        return pl.pallas_call(
            kernel,
            out_shape=[jax.ShapeDtypeStruct(b.shape, f32), jax.ShapeDtypeStruct((8, width), f32)],
            grid_spec=pltpu.PrefetchScalarGridSpec(
                num_scalar_prefetch=1, grid=(planes // pair,), in_specs=specs, out_specs=[two, fixed(8, width)]
            ),
            compiler_params=params(size),
            cost_estimate=pl.CostEstimate(
                flops=12 * chips * cores * width * b.size, bytes_accessed=b.size * 4 * (3 + 2 * chips), transcendentals=0
            ),
            name=name,
        )(core, *operands)

    operands = (early, *with_other(before), *with_other(after), u, part)
    steps, token = line_terms(early_kernel, "early_terms", 2, 60, [table(early)] + [two] * 6, operands)
    far_0, far_1 = follow("follow_early", far_0, far_1, after=token)
    operands = (late, *with_other(far_0), *with_other(far_1), u, steps)
    specs = [table(late)] + [in_lower] * 2 + [in_upper] * 2 + [two] * 2
    steps, _ = line_terms(functools.partial(late_kernel, half // pair), "late_terms", 1, 60, specs, operands)

    out = pl.pallas_call(
        functools.partial(last_kernel, planes),
        out_shape=jax.ShapeDtypeStruct(b.shape, f32),
        in_specs=[pl.BlockSpec(memory_space=pltpu.VMEM)] * 3,
        out_specs=in_memory,
        scratch_shapes=[pltpu.VMEM(b.shape, f32)]
        + [pltpu.SemaphoreType.DMA((1, planes)), pltpu.SemaphoreType.DMA((planes,))],
        compiler_params=params(8),
        cost_estimate=pl.CostEstimate(flops=2 * b.size, bytes_accessed=b.size * 16, transcendentals=0),
        name="last",
    )(time_term, inv, steps)
    return out[None]


def solution(mesh):
    spec = P("inst", "px", None, "pz")
    return jax.shard_map(on_device, mesh=mesh, in_specs=(spec,) * 5, out_specs=spec, check_vma=False)
```

```python
import functools
import math

import jax
import jax.numpy as jnp
import ml_dtypes
import numpy as np
from jax import lax
from jax.experimental import pallas as pl
from jax.experimental.pallas import tpu as pltpu
from jax.sharding import PartitionSpec as P

box_length = 4.0 * math.pi
diffusivity = 0.01
omega_tide = 4.0
coupling = 50.0
span_step = 0.05

f32 = jnp.float32
bf16 = jnp.bfloat16


def first_line(count):
    d = np.arange(count)
    sign = 1.0 - 2.0 * (d % 2)
    safe = np.where(d == 0, 1.0, np.tan(np.pi * d / count))
    return np.where(d == 0, 0.0, 0.5 * sign / safe)


def second_line(count):
    d = np.arange(count)
    sign = 1.0 - 2.0 * (d % 2)
    safe = np.where(d == 0, 1.0, np.sin(np.pi * d / count))
    return np.where(d == 0, -(count * count) / 12.0 - 1.0 / 6.0, -0.5 * sign / (safe * safe))


def wall_table(count):
    order = count - 1
    j = np.arange(count)
    angle = np.pi * j / order
    ends = (j == 0) | (j == order)
    c = np.where(ends, 2.0, 1.0) * (1.0 - 2.0 * (j % 2))
    total = j[:, None] + j[None, :]
    differ = j[:, None] - j[None, :]
    gap = -2.0 * np.sin(np.pi * total / (2 * order)) * np.sin(np.pi * differ / (2 * order))
    table = c[:, None] / c[None, :] / np.where(differ == 0, 1.0, gap)
    corner = (2.0 * order * order + 1.0) / 6.0
    sine_sq = np.where(ends, 1.0, np.sin(angle) ** 2)
    centre = -np.cos(angle) / (2.0 * sine_sq)
    centre[0], centre[order] = corner, -corner
    table = np.where(differ == 0, np.diag(centre), table)
    spacing = np.pi / order * (np.sin(angle) + np.pi / order)
    return table, spacing


def three_parts(table, axis):
    high = table.astype(np.float32).astype(ml_dtypes.bfloat16)
    low = (table - high.astype(np.float64)).astype(np.float32).astype(ml_dtypes.bfloat16)
    return np.concatenate([high, high, low], axis=axis)


def split(x):
    high = x.astype(bf16)
    return high, (x - high.astype(f32)).astype(bf16)


def derivatives(blocks, table):
    planes, rows, width = blocks[0].shape
    parts = [split(x.reshape(planes * rows, width)) for x in blocks]
    high, low = ([p[i] for p in parts] for i in range(2))
    both = jnp.dot(jnp.concatenate(high + low + high, axis=1), table, preferred_element_type=f32)
    return both[:, :width].reshape(planes, rows, width), both[:, width:].reshape(planes, rows, width)


def wall_kernel(dx, core_ref, wall_ref, line_ref, scale_ref, b_ref, edge_ref, other_ref, u_ref, v_ref, w_ref, n_ref, part_ref, inv_ref, token_ref):
    count, rows, width = b_ref.shape
    pair = u_ref.shape[0]
    start = pl.program_id(0) * pair
    here = b_ref[pl.ds(start, pair)]
    high, low = split(jnp.concatenate([here[i] for i in range(pair)], axis=1))
    both = jnp.dot(wall_ref[...], jnp.concatenate([high, low, high], axis=0), preferred_element_type=f32)
    grad_x, curv_x = derivatives([here, other_ref[...]], line_ref[0])
    for i in range(pair):
        z = start + i
        lanes = slice(i * width, (i + 1) * width)
        u, v, w = (r[i].astype(f32) for r in (u_ref, v_ref, w_ref))
        above = jnp.where(z == count - 1, edge_ref[0], b_ref[jnp.minimum(z + 1, count - 1)])
        below = jnp.where(z == 0, edge_ref[1], b_ref[jnp.maximum(z - 1, 0)])
        grad_z = (above - below) * (1.0 / (2.0 * span_step))
        curv_z = (above - 2.0 * here[i] + below) * (diffusivity / (span_step * span_step))
        radius = scale_ref[1] + jnp.abs(u) * (1.0 / dx) + jnp.abs(v) * scale_ref[0] + jnp.abs(w) * (1.0 / span_step)
        inv_ref[i] = 1.0 / radius
        advect = u * grad_x[i] + v * both[:rows, lanes] + w * grad_z
        part_ref[i] = -advect - (curv_x[i] + both[rows:, lanes] + curv_z) - coupling * n_ref[i]
    token_ref[...] = jnp.zeros_like(token_ref)


def early_kernel(core_ref, table_ref, *refs):
    blocks, (u_ref, part_ref, out_ref, token_ref) = refs[:4], refs[4:]
    grad_x, curv_x = derivatives([r[...] for r in blocks], table_ref[0])
    out_ref[...] = part_ref[...] - (u_ref[...].astype(f32) * grad_x + curv_x)
    token_ref[...] = jnp.zeros_like(token_ref)


def late_kernel(half, core_ref, table_ref, *refs):
    lower, upper = refs[:2], refs[2:4]
    u_ref, steps_ref, out_ref, token_ref = refs[4:]
    second = pl.program_id(0) >= half
    grad_x, curv_x = derivatives([jnp.where(second, y[...], x[...]) for x, y in zip(lower, upper)], table_ref[0])
    out_ref[...] = steps_ref[...] - (u_ref[...].astype(f32) * grad_x + curv_x)
    token_ref[...] = jnp.zeros_like(token_ref)


def halves_kernel(before_ref, after_ref, onward_ref, return_ref, held, in_sems, out_sems):
    half = onward_ref.shape[0]
    planes = [(before_ref.at[k], onward_ref.at[k]) for k in range(half)]
    planes += [(after_ref.at[half + k], return_ref.at[k]) for k in range(half)]
    come = [pltpu.make_async_copy(x, held.at[k], in_sems.at[k]) for k, (x, _) in enumerate(planes)]
    go = [pltpu.make_async_copy(held.at[k], y, out_sems.at[k]) for k, (_, y) in enumerate(planes)]
    for copy in come:
        copy.start()
    for first, second in zip(come, go):
        first.wait()
        second.start()
    for copy in go:
        copy.wait()


def follow_kernel(*refs):
    pass


def in_parts(count, sources, buffers, result, target, in_sems, out_sems, work):
    def part(k):
        return [pltpu.make_async_copy(x.at[at], y.at[at], in_sems.at[i, k]) for i, (x, y) in enumerate(zip(sources, buffers))]

    def out(k):
        return pltpu.make_async_copy(result.at[at], target.at[at], out_sems.at[k])

    for k in range(count):
        at = work.where(k)
        for copy in part(k):
            copy.start()
    for k in range(count):
        at = work.where(k)
        for copy in part(k):
            copy.wait()
        work.do(k)
        out(k).start()
    for k in range(count):
        at = work.where(k)
        out(k).wait()


class TimePart:
    def __init__(self, weights, order, size, source, result):
        self.weights, self.order, self.size, self.source, self.result = weights, order, size, source, result

    def where(self, k):
        return (slice(None), pl.ds(k * self.size, self.size))

    def do(self, k):
        weights, count = self.weights, self.source.shape[0]
        half = count // 2

        def body(step, carry):
            rows = pl.ds(pl.multiple_of(k * self.size + step * 8, 8), 8)
            b = [self.source[self.order.index(i), rows, :] for i in range(count)]
            totals = [weights[half] * b[(i + half) % count] for i in range(count)]
            for i in range(half):
                for d in range(1, half):
                    differ = b[(i + d) % count] - b[(i - d) % count]
                    totals[i] = totals[i] + weights[d] * differ
                    totals[i + half] = totals[i + half] - weights[half - d] * differ
            for i in range(count):
                self.result[self.order.index(i), rows, :] = totals[i]
            return carry

        lax.fori_loop(0, self.size // 8, body, 0)


class LastPart:
    def __init__(self, size, steps, time, inv, result):
        self.size, self.steps, self.time, self.inv, self.result = size, steps, time, inv, result

    def where(self, k):
        return (pl.ds(k * self.size, self.size),)

    def do(self, k):
        at = self.where(k)
        self.result[at] = (self.steps[at] - self.time[at]) * self.inv[at]


def time_kernel(weights, order, parts, in_ref, *refs):
    out_ref, source, result, in_sems, out_sems = refs[-5:]
    work = TimePart(weights, order, in_ref.shape[1] // parts, source, result)
    in_parts(parts, [in_ref], [source], result, out_ref, in_sems, out_sems, work)


def last_kernel(parts, time_ref, inv_ref, steps_ref, out_ref, result, in_sems, out_sems):
    work = LastPart(steps_ref.shape[0] // parts, steps_ref, time_ref, inv_ref, result)
    in_parts(parts, [], [], result, out_ref, in_sems, out_sems, work)


def on_device(stream_vel, normal_vel, span_vel, adjoint_buoy, adjoint_normal):
    _, planes, rows, width = adjoint_buoy.shape
    count_x, count_i, count_p = (lax.axis_size(a) for a in ("pz", "inst", "px"))
    full = width * count_x
    dx = box_length / full
    wave = 2.0 * math.pi / box_length

    cores = 2
    groups = (0,), (-1, 1), (2,)

    def line_table(core, chips):
        offsets = [cores * step + other - core for step in chips for other in (core, 1 - core)]
        k = np.concatenate([np.arange(width) + width * o for o in offsets])
        d = (np.arange(width)[None, :] - k[:, None]) % full
        table = np.concatenate([wave * first_line(full)[d], diffusivity * wave * wave * second_line(full)[d]], axis=1)
        return three_parts(table, 0)

    first, early, late = (jnp.asarray(np.stack([line_table(c, t) for c in range(cores)])) for t in groups)
    normal_table, spacing = wall_table(rows)
    wall = np.concatenate([normal_table, diffusivity * (normal_table @ normal_table)], axis=0)
    wall = jnp.asarray(three_parts(wall, 1))
    steady = 1.0 + omega_tide * count_i / 2.0 + 2.0 * diffusivity * (1.0 / dx**2 + 1.0 / spacing**2 + 1.0 / span_step**2)
    scale = np.stack([1.0 / spacing, steady]).astype(np.float32)[:, :, None]
    scale = np.broadcast_to(scale, (2, rows, width))
    weights = [float(x) for x in omega_tide * first_line(count_i)]

    core = (lax.axis_index("pz") % cores).astype(jnp.int32).reshape(1)

    b, u, v, w, n = (x[0] for x in (adjoint_buoy, stream_vel, normal_vel, span_vel, adjoint_normal))

    share = planes * rows // count_i
    turn = count_i // 2
    order = [j * 3 % turn + side * turn for j in range(turn) for side in range(2)]
    exchange = functools.partial(
        lax.all_to_all, axis_name="inst", split_axis=0, concat_axis=0, axis_index_groups=[order], tiled=True
    )
    sent = exchange(b.reshape(count_i, share, width))

    members = range(count_x)
    onward = [(i, (i + cores) % count_x) for i in members]
    return_ = [(j, i) for i, j in onward]
    partner = [(i, i ^ 1) for i in members]
    half = planes // 2
    before = lax.ppermute(b, "pz", onward)
    after = lax.ppermute(b, "pz", return_)
    other = lax.ppermute(b, "pz", partner)
    swap = [(i, (i + 1) % count_p) for i in range(count_p)]
    back = [(j, i) for i, j in swap]
    if count_p == 2:
        edge = lax.ppermute(jnp.stack([b[0], b[planes - 1]]), "px", swap)
    else:
        edge = jnp.stack([lax.ppermute(b[0], "px", back), lax.ppermute(b[planes - 1], "px", swap)])

    pair = 2
    anywhere, in_memory = pl.BlockSpec(memory_space=pl.ANY), pl.BlockSpec(memory_space=pltpu.HBM)
    params = lambda size: pltpu.CompilerParams(vmem_limit_bytes=size * 2**20)
    spec = lambda f: pl.BlockSpec((pair, rows, width), lambda s, c: (f(s), 0, 0))
    two = spec(lambda s: s)
    fixed = lambda *shape: pl.BlockSpec(shape, lambda s, c: (0,) * len(shape))
    table = lambda t: pl.BlockSpec((1,) + t.shape[1:], lambda s, c: (c[0], 0, 0))
    part, inv, token = pl.pallas_call(
        functools.partial(wall_kernel, dx),
        out_shape=[jax.ShapeDtypeStruct(b.shape, f32)] * 2 + [jax.ShapeDtypeStruct((8, width), f32)],
        grid_spec=pltpu.PrefetchScalarGridSpec(
            num_scalar_prefetch=1,
            grid=(planes // pair,),
            in_specs=[fixed(*wall.shape), table(first), fixed(*scale.shape), fixed(*b.shape), fixed(2, rows, width)] + [two] * 5,
            out_specs=[two] * 2 + [fixed(8, width)],
        ),
        compiler_params=params(24),
        cost_estimate=pl.CostEstimate(flops=16 * rows * b.size, bytes_accessed=b.size * 28, transcendentals=0),
        name="wall_terms",
    )(core, wall, first, jnp.asarray(scale), b, edge, other, u, v, w, n)

    def follow(name, *arrays, after):
        return pl.pallas_call(
            follow_kernel,
            out_shape=[jax.ShapeDtypeStruct(x.shape, f32) for x in arrays],
            in_specs=[anywhere] * (len(arrays) + 1),
            out_specs=[anywhere] * len(arrays),
            input_output_aliases={i: i for i in range(len(arrays))},
            compiler_params=params(1),
            name=name,
        )(*arrays, after)

    onward_half, return_half = pl.pallas_call(
        halves_kernel,
        out_shape=[jax.ShapeDtypeStruct((half, rows, width), f32)] * 2,
        in_specs=[anywhere] * 2,
        out_specs=[anywhere] * 2,
        scratch_shapes=[pltpu.VMEM(b.shape, f32)] + [pltpu.SemaphoreType.DMA((2 * half,))] * 2,
        compiler_params=params(8),
        cost_estimate=pl.CostEstimate(flops=0, bytes_accessed=b.size * 8, transcendentals=0),
        name="halves",
    )(before, after)
    far_0 = lax.ppermute(onward_half, "pz", onward)
    far_1 = lax.ppermute(return_half, "pz", return_)

    parts = 8
    applied = pl.pallas_call(
        functools.partial(time_kernel, weights, order, parts),
        out_shape=jax.ShapeDtypeStruct(sent.shape, f32),
        in_specs=[in_memory, anywhere],
        out_specs=in_memory,
        scratch_shapes=[pltpu.VMEM(sent.shape, f32)] * 2
        + [pltpu.SemaphoreType.DMA((1, parts)), pltpu.SemaphoreType.DMA((parts,))],
        compiler_params=params(60),
        cost_estimate=pl.CostEstimate(flops=sent.size * 16, bytes_accessed=sent.size * 8, transcendentals=0),
        name="time_term",
    )(sent, token)
    time_term = exchange(applied).reshape(planes, rows, width)

    with_other = lambda r: (r, lax.ppermute(r, "pz", partner))
    last_low = half // pair - 1
    in_lower, in_upper = spec(lambda s: jnp.minimum(s, last_low)), spec(lambda s: jnp.maximum(s - last_low - 1, 0))

    def line_terms(kernel, name, chips, size, specs, operands):
        return pl.pallas_call(
            kernel,
            out_shape=[jax.ShapeDtypeStruct(b.shape, f32), jax.ShapeDtypeStruct((8, width), f32)],
            grid_spec=pltpu.PrefetchScalarGridSpec(
                num_scalar_prefetch=1, grid=(planes // pair,), in_specs=specs, out_specs=[two, fixed(8, width)]
            ),
            compiler_params=params(size),
            cost_estimate=pl.CostEstimate(
                flops=12 * chips * cores * width * b.size, bytes_accessed=b.size * 4 * (3 + 2 * chips), transcendentals=0
            ),
            name=name,
        )(core, *operands)

    operands = (early, *with_other(before), *with_other(after), u, part)
    steps, token = line_terms(early_kernel, "early_terms", 2, 60, [table(early)] + [two] * 6, operands)
    far_0, far_1 = follow("follow_early", far_0, far_1, after=token)
    operands = (late, *with_other(far_0), *with_other(far_1), u, steps)
    specs = [table(late)] + [in_lower] * 2 + [in_upper] * 2 + [two] * 2
    steps, _ = line_terms(functools.partial(late_kernel, half // pair), "late_terms", 1, 60, specs, operands)

    out = pl.pallas_call(
        functools.partial(last_kernel, planes),
        out_shape=jax.ShapeDtypeStruct(b.shape, f32),
        in_specs=[pl.BlockSpec(memory_space=pltpu.VMEM)] * 3,
        out_specs=in_memory,
        scratch_shapes=[pltpu.VMEM(b.shape, f32)]
        + [pltpu.SemaphoreType.DMA((1, planes)), pltpu.SemaphoreType.DMA((planes,))],
        compiler_params=params(8),
        cost_estimate=pl.CostEstimate(flops=2 * b.size, bytes_accessed=b.size * 16, transcendentals=0),
        name="last",
    )(time_term, inv, steps)
    return out[None]


def solution(mesh):
    spec = P("inst", "px", None, "pz")
    return jax.shard_map(on_device, mesh=mesh, in_specs=(spec,) * 5, out_specs=spec, check_vma=False)
```

```python
import functools
import math

import jax
import jax.numpy as jnp
import ml_dtypes
import numpy as np
from jax import lax
from jax.experimental import pallas as pl
from jax.experimental.pallas import tpu as pltpu
from jax.sharding import PartitionSpec as P

box_length = 4.0 * math.pi
diffusivity = 0.01
omega_tide = 4.0
coupling = 50.0
span_step = 0.05

f32 = jnp.float32
bf16 = jnp.bfloat16


def first_line(count):
    d = np.arange(count)
    sign = 1.0 - 2.0 * (d % 2)
    safe = np.where(d == 0, 1.0, np.tan(np.pi * d / count))
    return np.where(d == 0, 0.0, 0.5 * sign / safe)


def second_line(count):
    d = np.arange(count)
    sign = 1.0 - 2.0 * (d % 2)
    safe = np.where(d == 0, 1.0, np.sin(np.pi * d / count))
    return np.where(d == 0, -(count * count) / 12.0 - 1.0 / 6.0, -0.5 * sign / (safe * safe))


def wall_table(count):
    order = count - 1
    j = np.arange(count)
    angle = np.pi * j / order
    ends = (j == 0) | (j == order)
    c = np.where(ends, 2.0, 1.0) * (1.0 - 2.0 * (j % 2))
    total = j[:, None] + j[None, :]
    differ = j[:, None] - j[None, :]
    gap = -2.0 * np.sin(np.pi * total / (2 * order)) * np.sin(np.pi * differ / (2 * order))
    table = c[:, None] / c[None, :] / np.where(differ == 0, 1.0, gap)
    corner = (2.0 * order * order + 1.0) / 6.0
    sine_sq = np.where(ends, 1.0, np.sin(angle) ** 2)
    centre = -np.cos(angle) / (2.0 * sine_sq)
    centre[0], centre[order] = corner, -corner
    table = np.where(differ == 0, np.diag(centre), table)
    spacing = np.pi / order * (np.sin(angle) + np.pi / order)
    return table, spacing


def three_parts(table, axis):
    high = table.astype(np.float32).astype(ml_dtypes.bfloat16)
    low = (table - high.astype(np.float64)).astype(np.float32).astype(ml_dtypes.bfloat16)
    return np.concatenate([high, high, low], axis=axis)


def split(x):
    high = x.astype(bf16)
    return high, (x - high.astype(f32)).astype(bf16)


def derivatives(blocks, table):
    planes, rows, width = blocks[0].shape
    parts = [split(x.reshape(planes * rows, width)) for x in blocks]
    high, low = ([p[i] for p in parts] for i in range(2))
    both = jnp.dot(jnp.concatenate(high + low + high, axis=1), table, preferred_element_type=f32)
    return both[:, :width].reshape(planes, rows, width), both[:, width:].reshape(planes, rows, width)


def wall_kernel(dx, core_ref, wall_ref, line_ref, scale_ref, b_ref, edge_ref, other_ref, u_ref, v_ref, w_ref, n_ref, part_ref, inv_ref, token_ref):
    count, rows, width = b_ref.shape
    pair = u_ref.shape[0]
    start = pl.program_id(0) * pair
    here = b_ref[pl.ds(start, pair)]
    high, low = split(jnp.concatenate([here[i] for i in range(pair)], axis=1))
    both = jnp.dot(wall_ref[...], jnp.concatenate([high, low, high], axis=0), preferred_element_type=f32)
    grad_x, curv_x = derivatives([here, other_ref[...]], line_ref[0])
    for i in range(pair):
        z = start + i
        lanes = slice(i * width, (i + 1) * width)
        u, v, w = (r[i].astype(f32) for r in (u_ref, v_ref, w_ref))
        above = jnp.where(z == count - 1, edge_ref[0], b_ref[jnp.minimum(z + 1, count - 1)])
        below = jnp.where(z == 0, edge_ref[1], b_ref[jnp.maximum(z - 1, 0)])
        grad_z = (above - below) * (1.0 / (2.0 * span_step))
        curv_z = (above - 2.0 * here[i] + below) * (diffusivity / (span_step * span_step))
        radius = scale_ref[1] + jnp.abs(u) * (1.0 / dx) + jnp.abs(v) * scale_ref[0] + jnp.abs(w) * (1.0 / span_step)
        inv_ref[i] = 1.0 / radius
        advect = u * grad_x[i] + v * both[:rows, lanes] + w * grad_z
        part_ref[i] = -advect - (curv_x[i] + both[rows:, lanes] + curv_z) - coupling * n_ref[i]
    token_ref[...] = jnp.zeros_like(token_ref)


def early_kernel(core_ref, table_ref, *refs):
    blocks, (u_ref, part_ref, out_ref, token_ref) = refs[:4], refs[4:]
    grad_x, curv_x = derivatives([r[...] for r in blocks], table_ref[0])
    out_ref[...] = part_ref[...] - (u_ref[...].astype(f32) * grad_x + curv_x)
    token_ref[...] = jnp.zeros_like(token_ref)


def late_kernel(half, core_ref, table_ref, *refs):
    lower, upper = refs[:2], refs[2:4]
    u_ref, steps_ref, out_ref, token_ref = refs[4:]
    second = pl.program_id(0) >= half
    grad_x, curv_x = derivatives([jnp.where(second, y[...], x[...]) for x, y in zip(lower, upper)], table_ref[0])
    out_ref[...] = steps_ref[...] - (u_ref[...].astype(f32) * grad_x + curv_x)
    token_ref[...] = jnp.zeros_like(token_ref)


def halves_kernel(before_ref, after_ref, onward_ref, return_ref, held, in_sems, out_sems):
    half = onward_ref.shape[0]
    planes = [(before_ref.at[k], onward_ref.at[k]) for k in range(half)]
    planes += [(after_ref.at[half + k], return_ref.at[k]) for k in range(half)]
    come = [pltpu.make_async_copy(x, held.at[k], in_sems.at[k]) for k, (x, _) in enumerate(planes)]
    go = [pltpu.make_async_copy(held.at[k], y, out_sems.at[k]) for k, (_, y) in enumerate(planes)]
    for copy in come:
        copy.start()
    for first, second in zip(come, go):
        first.wait()
        second.start()
    for copy in go:
        copy.wait()


def follow_kernel(*refs):
    pass


def in_parts(count, sources, buffers, result, target, in_sems, out_sems, work):
    def part(k):
        return [pltpu.make_async_copy(x.at[at], y.at[at], in_sems.at[i, k]) for i, (x, y) in enumerate(zip(sources, buffers))]

    def out(k):
        return pltpu.make_async_copy(result.at[at], target.at[at], out_sems.at[k])

    for k in range(count):
        at = work.where(k)
        for copy in part(k):
            copy.start()
    for k in range(count):
        at = work.where(k)
        for copy in part(k):
            copy.wait()
        work.do(k)
        out(k).start()
    for k in range(count):
        at = work.where(k)
        out(k).wait()


class TimePart:
    def __init__(self, weights, size, source, result):
        self.weights, self.size, self.source, self.result = weights, size, source, result

    def where(self, k):
        return (slice(None), pl.ds(k * self.size, self.size))

    def do(self, k):
        weights, count = self.weights, self.source.shape[0]
        half = count // 2

        def body(step, carry):
            rows = pl.ds(pl.multiple_of(k * self.size + step * 8, 8), 8)
            b = [self.source[i, rows, :] for i in range(count)]
            totals = [weights[half] * b[(i + half) % count] for i in range(count)]
            for i in range(half):
                for d in range(1, half):
                    differ = b[(i + d) % count] - b[(i - d) % count]
                    totals[i] = totals[i] + weights[d] * differ
                    totals[i + half] = totals[i + half] - weights[half - d] * differ
            for i in range(count):
                self.result[i, rows, :] = totals[i]
            return carry

        lax.fori_loop(0, self.size // 8, body, 0)


class LastPart:
    def __init__(self, size, steps, time, inv, result):
        self.size, self.steps, self.time, self.inv, self.result = size, steps, time, inv, result

    def where(self, k):
        return (pl.ds(k * self.size, self.size),)

    def do(self, k):
        at = self.where(k)
        self.result[at] = (self.steps[at] - self.time[at]) * self.inv[at]


def time_kernel(weights, parts, in_ref, *refs):
    out_ref, source, result, in_sems, out_sems = refs[-5:]
    work = TimePart(weights, in_ref.shape[1] // parts, source, result)
    in_parts(parts, [in_ref], [source], result, out_ref, in_sems, out_sems, work)


def last_kernel(parts, time_ref, inv_ref, steps_ref, out_ref, result, in_sems, out_sems):
    work = LastPart(steps_ref.shape[0] // parts, steps_ref, time_ref, inv_ref, result)
    in_parts(parts, [], [], result, out_ref, in_sems, out_sems, work)


def on_device(stream_vel, normal_vel, span_vel, adjoint_buoy, adjoint_normal):
    _, planes, rows, width = adjoint_buoy.shape
    count_x, count_i, count_p = (lax.axis_size(a) for a in ("pz", "inst", "px"))
    full = width * count_x
    dx = box_length / full
    wave = 2.0 * math.pi / box_length

    cores = 2
    groups = (0,), (-1, 1), (2,)

    def line_table(core, chips):
        offsets = [cores * step + other - core for step in chips for other in (core, 1 - core)]
        k = np.concatenate([np.arange(width) + width * o for o in offsets])
        d = (np.arange(width)[None, :] - k[:, None]) % full
        table = np.concatenate([wave * first_line(full)[d], diffusivity * wave * wave * second_line(full)[d]], axis=1)
        return three_parts(table, 0)

    first, early, late = (jnp.asarray(np.stack([line_table(c, t) for c in range(cores)])) for t in groups)
    normal_table, spacing = wall_table(rows)
    wall = np.concatenate([normal_table, diffusivity * (normal_table @ normal_table)], axis=0)
    wall = jnp.asarray(three_parts(wall, 1))
    steady = 1.0 + omega_tide * count_i / 2.0 + 2.0 * diffusivity * (1.0 / dx**2 + 1.0 / spacing**2 + 1.0 / span_step**2)
    scale = np.stack([1.0 / spacing, steady]).astype(np.float32)[:, :, None]
    scale = np.broadcast_to(scale, (2, rows, width))
    weights = [float(x) for x in omega_tide * first_line(count_i)]

    core = (lax.axis_index("pz") % cores).astype(jnp.int32).reshape(1)

    b, u, v, w, n = (x[0] for x in (adjoint_buoy, stream_vel, normal_vel, span_vel, adjoint_normal))

    share = planes * rows // count_i
    exchange = functools.partial(lax.all_to_all, axis_name="inst", split_axis=0, concat_axis=0, tiled=True)
    sent = exchange(b.reshape(count_i, share, width))

    members = range(count_x)
    onward = [(i, (i + cores) % count_x) for i in members]
    return_ = [(j, i) for i, j in onward]
    partner = [(i, i ^ 1) for i in members]
    half = planes // 2
    before = lax.ppermute(b, "pz", onward)
    after = lax.ppermute(b, "pz", return_)
    other = lax.ppermute(b, "pz", partner)
    swap = [(i, (i + 1) % count_p) for i in range(count_p)]
    back = [(j, i) for i, j in swap]
    if count_p == 2:
        edge = lax.ppermute(jnp.stack([b[0], b[planes - 1]]), "px", swap)
    else:
        edge = jnp.stack([lax.ppermute(b[0], "px", back), lax.ppermute(b[planes - 1], "px", swap)])

    pair = 2
    anywhere, in_memory = pl.BlockSpec(memory_space=pl.ANY), pl.BlockSpec(memory_space=pltpu.HBM)
    params = lambda size: pltpu.CompilerParams(vmem_limit_bytes=size * 2**20)
    spec = lambda f: pl.BlockSpec((pair, rows, width), lambda s, c: (f(s), 0, 0))
    two = spec(lambda s: s)
    fixed = lambda *shape: pl.BlockSpec(shape, lambda s, c: (0,) * len(shape))
    table = lambda t: pl.BlockSpec((1,) + t.shape[1:], lambda s, c: (c[0], 0, 0))
    part, inv, token = pl.pallas_call(
        functools.partial(wall_kernel, dx),
        out_shape=[jax.ShapeDtypeStruct(b.shape, f32)] * 2 + [jax.ShapeDtypeStruct((8, width), f32)],
        grid_spec=pltpu.PrefetchScalarGridSpec(
            num_scalar_prefetch=1,
            grid=(planes // pair,),
            in_specs=[fixed(*wall.shape), table(first), fixed(*scale.shape), fixed(*b.shape), fixed(2, rows, width)] + [two] * 5,
            out_specs=[two] * 2 + [fixed(8, width)],
        ),
        compiler_params=params(24),
        cost_estimate=pl.CostEstimate(flops=16 * rows * b.size, bytes_accessed=b.size * 28, transcendentals=0),
        name="wall_terms",
    )(core, wall, first, jnp.asarray(scale), b, edge, other, u, v, w, n)

    def follow(name, *arrays, after):
        return pl.pallas_call(
            follow_kernel,
            out_shape=[jax.ShapeDtypeStruct(x.shape, f32) for x in arrays],
            in_specs=[anywhere] * (len(arrays) + 1),
            out_specs=[anywhere] * len(arrays),
            input_output_aliases={i: i for i in range(len(arrays))},
            compiler_params=params(1),
            name=name,
        )(*arrays, after)

    onward_half, return_half = pl.pallas_call(
        halves_kernel,
        out_shape=[jax.ShapeDtypeStruct((half, rows, width), f32)] * 2,
        in_specs=[anywhere] * 2,
        out_specs=[anywhere] * 2,
        scratch_shapes=[pltpu.VMEM(b.shape, f32)] + [pltpu.SemaphoreType.DMA((2 * half,))] * 2,
        compiler_params=params(8),
        cost_estimate=pl.CostEstimate(flops=0, bytes_accessed=b.size * 8, transcendentals=0),
        name="halves",
    )(before, after)
    far_0 = lax.ppermute(onward_half, "pz", onward)
    far_1 = lax.ppermute(return_half, "pz", return_)

    parts = 8
    applied = pl.pallas_call(
        functools.partial(time_kernel, weights, parts),
        out_shape=jax.ShapeDtypeStruct(sent.shape, f32),
        in_specs=[in_memory, anywhere],
        out_specs=in_memory,
        scratch_shapes=[pltpu.VMEM(sent.shape, f32)] * 2
        + [pltpu.SemaphoreType.DMA((1, parts)), pltpu.SemaphoreType.DMA((parts,))],
        compiler_params=params(60),
        cost_estimate=pl.CostEstimate(flops=sent.size * 16, bytes_accessed=sent.size * 8, transcendentals=0),
        name="time_term",
    )(sent, token)
    time_term = exchange(applied).reshape(planes, rows, width)

    with_other = lambda r: (r, lax.ppermute(r, "pz", partner))
    last_low = half // pair - 1
    in_lower, in_upper = spec(lambda s: jnp.minimum(s, last_low)), spec(lambda s: jnp.maximum(s - last_low - 1, 0))

    def line_terms(kernel, name, chips, size, specs, operands):
        return pl.pallas_call(
            kernel,
            out_shape=[jax.ShapeDtypeStruct(b.shape, f32), jax.ShapeDtypeStruct((8, width), f32)],
            grid_spec=pltpu.PrefetchScalarGridSpec(
                num_scalar_prefetch=1, grid=(planes // pair,), in_specs=specs, out_specs=[two, fixed(8, width)]
            ),
            compiler_params=params(size),
            cost_estimate=pl.CostEstimate(
                flops=12 * chips * cores * width * b.size, bytes_accessed=b.size * 4 * (3 + 2 * chips), transcendentals=0
            ),
            name=name,
        )(core, *operands)

    operands = (early, *with_other(before), *with_other(after), u, part)
    steps, token = line_terms(early_kernel, "early_terms", 2, 40, [table(early)] + [two] * 6, operands)
    far_0, far_1 = follow("follow_early", far_0, far_1, after=token)
    operands = (late, *with_other(far_0), *with_other(far_1), u, steps)
    specs = [table(late)] + [in_lower] * 2 + [in_upper] * 2 + [two] * 2
    steps, _ = line_terms(functools.partial(late_kernel, half // pair), "late_terms", 1, 40, specs, operands)

    out = pl.pallas_call(
        functools.partial(last_kernel, planes),
        out_shape=jax.ShapeDtypeStruct(b.shape, f32),
        in_specs=[pl.BlockSpec(memory_space=pltpu.VMEM)] * 3,
        out_specs=in_memory,
        scratch_shapes=[pltpu.VMEM(b.shape, f32)]
        + [pltpu.SemaphoreType.DMA((1, planes)), pltpu.SemaphoreType.DMA((planes,))],
        compiler_params=params(8),
        cost_estimate=pl.CostEstimate(flops=2 * b.size, bytes_accessed=b.size * 16, transcendentals=0),
        name="last",
    )(time_term, inv, steps)
    return out[None]


def solution(mesh):
    spec = P("inst", "px", None, "pz")
    return jax.shard_map(on_device, mesh=mesh, in_specs=(spec,) * 5, out_specs=spec, check_vma=False)
```

```python
import functools
import math

import jax
import jax.numpy as jnp
import ml_dtypes
import numpy as np
from jax import lax
from jax.experimental import pallas as pl
from jax.experimental.pallas import tpu as pltpu
from jax.sharding import PartitionSpec as P

box_length = 4.0 * math.pi
diffusivity = 0.01
omega_tide = 4.0
coupling = 50.0
span_step = 0.05

f32 = jnp.float32
bf16 = jnp.bfloat16


def first_line(count):
    d = np.arange(count)
    sign = 1.0 - 2.0 * (d % 2)
    safe = np.where(d == 0, 1.0, np.tan(np.pi * d / count))
    return np.where(d == 0, 0.0, 0.5 * sign / safe)


def second_line(count):
    d = np.arange(count)
    sign = 1.0 - 2.0 * (d % 2)
    safe = np.where(d == 0, 1.0, np.sin(np.pi * d / count))
    return np.where(d == 0, -(count * count) / 12.0 - 1.0 / 6.0, -0.5 * sign / (safe * safe))


def wall_table(count):
    order = count - 1
    j = np.arange(count)
    angle = np.pi * j / order
    ends = (j == 0) | (j == order)
    c = np.where(ends, 2.0, 1.0) * (1.0 - 2.0 * (j % 2))
    total = j[:, None] + j[None, :]
    differ = j[:, None] - j[None, :]
    gap = -2.0 * np.sin(np.pi * total / (2 * order)) * np.sin(np.pi * differ / (2 * order))
    table = c[:, None] / c[None, :] / np.where(differ == 0, 1.0, gap)
    corner = (2.0 * order * order + 1.0) / 6.0
    sine_sq = np.where(ends, 1.0, np.sin(angle) ** 2)
    centre = -np.cos(angle) / (2.0 * sine_sq)
    centre[0], centre[order] = corner, -corner
    table = np.where(differ == 0, np.diag(centre), table)
    spacing = np.pi / order * (np.sin(angle) + np.pi / order)
    return table, spacing


def three_parts(table, axis):
    high = table.astype(np.float32).astype(ml_dtypes.bfloat16)
    low = (table - high.astype(np.float64)).astype(np.float32).astype(ml_dtypes.bfloat16)
    return np.concatenate([high, high, low], axis=axis)


def split(x):
    high = x.astype(bf16)
    return high, (x - high.astype(f32)).astype(bf16)


def derivatives(blocks, table):
    planes, rows, width = blocks[0].shape
    parts = [split(x.reshape(planes * rows, width)) for x in blocks]
    high, low = ([p[i] for p in parts] for i in range(2))
    both = jnp.dot(jnp.concatenate(high + low + high, axis=1), table, preferred_element_type=f32)
    return both[:, :width].reshape(planes, rows, width), both[:, width:].reshape(planes, rows, width)


def wall_kernel(dx, core_ref, wall_ref, line_ref, scale_ref, b_ref, edge_ref, other_ref, u_ref, v_ref, w_ref, n_ref, part_ref, inv_ref, token_ref):
    count, rows, width = b_ref.shape
    pair = u_ref.shape[0]
    start = pl.program_id(0) * pair
    here = b_ref[pl.ds(start, pair)]
    high, low = split(jnp.concatenate([here[i] for i in range(pair)], axis=1))
    both = jnp.dot(wall_ref[...], jnp.concatenate([high, low, high], axis=0), preferred_element_type=f32)
    grad_x, curv_x = derivatives([here, other_ref[...]], line_ref[0])
    for i in range(pair):
        z = start + i
        lanes = slice(i * width, (i + 1) * width)
        u, v, w = (r[i].astype(f32) for r in (u_ref, v_ref, w_ref))
        above = jnp.where(z == count - 1, edge_ref[0], b_ref[jnp.minimum(z + 1, count - 1)])
        below = jnp.where(z == 0, edge_ref[1], b_ref[jnp.maximum(z - 1, 0)])
        grad_z = (above - below) * (1.0 / (2.0 * span_step))
        curv_z = (above - 2.0 * here[i] + below) * (diffusivity / (span_step * span_step))
        radius = scale_ref[1] + jnp.abs(u) * (1.0 / dx) + jnp.abs(v) * scale_ref[0] + jnp.abs(w) * (1.0 / span_step)
        inv_ref[i] = 1.0 / radius
        advect = u * grad_x[i] + v * both[:rows, lanes] + w * grad_z
        part_ref[i] = -advect - (curv_x[i] + both[rows:, lanes] + curv_z) - coupling * n_ref[i]
    token_ref[...] = jnp.zeros_like(token_ref)


def early_kernel(core_ref, table_ref, *refs):
    blocks, (u_ref, part_ref, out_ref, token_ref) = refs[:4], refs[4:]
    grad_x, curv_x = derivatives([r[...] for r in blocks], table_ref[0])
    out_ref[...] = part_ref[...] - (u_ref[...].astype(f32) * grad_x + curv_x)
    token_ref[...] = jnp.zeros_like(token_ref)


def late_kernel(half, core_ref, table_ref, *refs):
    lower, upper = refs[:2], refs[2:4]
    u_ref, steps_ref, out_ref, token_ref = refs[4:]
    second = pl.program_id(0) >= half
    grad_x, curv_x = derivatives([jnp.where(second, y[...], x[...]) for x, y in zip(lower, upper)], table_ref[0])
    out_ref[...] = steps_ref[...] - (u_ref[...].astype(f32) * grad_x + curv_x)
    token_ref[...] = jnp.zeros_like(token_ref)


def halves_kernel(before_ref, after_ref, onward_ref, return_ref, held, in_sems, out_sems):
    half = onward_ref.shape[0]
    planes = [(before_ref.at[k], onward_ref.at[k]) for k in range(half)]
    planes += [(after_ref.at[half + k], return_ref.at[k]) for k in range(half)]
    come = [pltpu.make_async_copy(x, held.at[k], in_sems.at[k]) for k, (x, _) in enumerate(planes)]
    go = [pltpu.make_async_copy(held.at[k], y, out_sems.at[k]) for k, (_, y) in enumerate(planes)]
    for copy in come:
        copy.start()
    for first, second in zip(come, go):
        first.wait()
        second.start()
    for copy in go:
        copy.wait()


def follow_kernel(*refs):
    pass


def in_parts(count, sources, buffers, result, target, in_sems, out_sems, work):
    def part(k):
        return [pltpu.make_async_copy(x.at[at], y.at[at], in_sems.at[i, k]) for i, (x, y) in enumerate(zip(sources, buffers))]

    def out(k):
        return pltpu.make_async_copy(result.at[at], target.at[at], out_sems.at[k])

    for k in range(count):
        at = work.where(k)
        for copy in part(k):
            copy.start()
    for k in range(count):
        at = work.where(k)
        for copy in part(k):
            copy.wait()
        work.do(k)
        out(k).start()
    for k in range(count):
        at = work.where(k)
        out(k).wait()


class TimePart:
    def __init__(self, weights, size, source, result):
        self.weights, self.size, self.source, self.result = weights, size, source, result

    def where(self, k):
        return (slice(None), pl.ds(k * self.size, self.size))

    def do(self, k):
        weights, count = self.weights, self.source.shape[0]
        half = count // 2

        def body(step, carry):
            rows = pl.ds(pl.multiple_of(k * self.size + step * 8, 8), 8)
            b = [self.source[i, rows, :] for i in range(count)]
            totals = [weights[half] * b[(i + half) % count] for i in range(count)]
            for i in range(half):
                for d in range(1, half):
                    differ = b[(i + d) % count] - b[(i - d) % count]
                    totals[i] = totals[i] + weights[d] * differ
                    totals[i + half] = totals[i + half] - weights[half - d] * differ
            for i in range(count):
                self.result[i, rows, :] = totals[i]
            return carry

        lax.fori_loop(0, self.size // 8, body, 0)


class LastPart:
    def __init__(self, size, steps, time, inv, result):
        self.size, self.steps, self.time, self.inv, self.result = size, steps, time, inv, result

    def where(self, k):
        return (pl.ds(k * self.size, self.size),)

    def do(self, k):
        at = self.where(k)
        self.result[at] = (self.steps[at] - self.time[at]) * self.inv[at]


def time_kernel(weights, parts, in_ref, *refs):
    out_ref, source, result, in_sems, out_sems = refs[-5:]
    work = TimePart(weights, in_ref.shape[1] // parts, source, result)
    in_parts(parts, [in_ref], [source], result, out_ref, in_sems, out_sems, work)


def last_kernel(parts, inv_ref, time_ref, steps_ref, out_ref, time, steps, result, in_sems, out_sems):
    work = LastPart(steps_ref.shape[0] // parts, steps, time, inv_ref, result)
    in_parts(parts, [time_ref, steps_ref], [time, steps], result, out_ref, in_sems, out_sems, work)


def on_device(stream_vel, normal_vel, span_vel, adjoint_buoy, adjoint_normal):
    _, planes, rows, width = adjoint_buoy.shape
    count_x, count_i, count_p = (lax.axis_size(a) for a in ("pz", "inst", "px"))
    full = width * count_x
    dx = box_length / full
    wave = 2.0 * math.pi / box_length

    cores = 2
    groups = (0,), (-1, 1), (2,)

    def line_table(core, chips):
        offsets = [cores * step + other - core for step in chips for other in (core, 1 - core)]
        k = np.concatenate([np.arange(width) + width * o for o in offsets])
        d = (np.arange(width)[None, :] - k[:, None]) % full
        table = np.concatenate([wave * first_line(full)[d], diffusivity * wave * wave * second_line(full)[d]], axis=1)
        return three_parts(table, 0)

    first, early, late = (jnp.asarray(np.stack([line_table(c, t) for c in range(cores)])) for t in groups)
    normal_table, spacing = wall_table(rows)
    wall = np.concatenate([normal_table, diffusivity * (normal_table @ normal_table)], axis=0)
    wall = jnp.asarray(three_parts(wall, 1))
    steady = 1.0 + omega_tide * count_i / 2.0 + 2.0 * diffusivity * (1.0 / dx**2 + 1.0 / spacing**2 + 1.0 / span_step**2)
    scale = np.stack([1.0 / spacing, steady]).astype(np.float32)[:, :, None]
    scale = np.broadcast_to(scale, (2, rows, width))
    weights = [float(x) for x in omega_tide * first_line(count_i)]

    core = (lax.axis_index("pz") % cores).astype(jnp.int32).reshape(1)

    b, u, v, w, n = (x[0] for x in (adjoint_buoy, stream_vel, normal_vel, span_vel, adjoint_normal))

    share = planes * rows // count_i
    exchange = functools.partial(lax.all_to_all, axis_name="inst", split_axis=0, concat_axis=0, tiled=True)
    sent = exchange(b.reshape(count_i, share, width))

    members = range(count_x)
    onward = [(i, (i + cores) % count_x) for i in members]
    return_ = [(j, i) for i, j in onward]
    partner = [(i, i ^ 1) for i in members]
    half = planes // 2
    before = lax.ppermute(b, "pz", onward)
    after = lax.ppermute(b, "pz", return_)
    other = lax.ppermute(b, "pz", partner)
    swap = [(i, (i + 1) % count_p) for i in range(count_p)]
    back = [(j, i) for i, j in swap]
    if count_p == 2:
        edge = lax.ppermute(jnp.stack([b[0], b[planes - 1]]), "px", swap)
    else:
        edge = jnp.stack([lax.ppermute(b[0], "px", back), lax.ppermute(b[planes - 1], "px", swap)])

    pair = 2
    anywhere, in_memory = pl.BlockSpec(memory_space=pl.ANY), pl.BlockSpec(memory_space=pltpu.HBM)
    params = lambda size: pltpu.CompilerParams(vmem_limit_bytes=size * 2**20)
    spec = lambda f: pl.BlockSpec((pair, rows, width), lambda s, c: (f(s), 0, 0))
    two = spec(lambda s: s)
    fixed = lambda *shape: pl.BlockSpec(shape, lambda s, c: (0,) * len(shape))
    table = lambda t: pl.BlockSpec((1,) + t.shape[1:], lambda s, c: (c[0], 0, 0))
    part, inv, token = pl.pallas_call(
        functools.partial(wall_kernel, dx),
        out_shape=[jax.ShapeDtypeStruct(b.shape, f32)] * 2 + [jax.ShapeDtypeStruct((8, width), f32)],
        grid_spec=pltpu.PrefetchScalarGridSpec(
            num_scalar_prefetch=1,
            grid=(planes // pair,),
            in_specs=[fixed(*wall.shape), table(first), fixed(*scale.shape), fixed(*b.shape), fixed(2, rows, width)] + [two] * 5,
            out_specs=[two] * 2 + [fixed(8, width)],
        ),
        compiler_params=params(24),
        cost_estimate=pl.CostEstimate(flops=16 * rows * b.size, bytes_accessed=b.size * 28, transcendentals=0),
        name="wall_terms",
    )(core, wall, first, jnp.asarray(scale), b, edge, other, u, v, w, n)

    def follow(name, *arrays, after):
        return pl.pallas_call(
            follow_kernel,
            out_shape=[jax.ShapeDtypeStruct(x.shape, f32) for x in arrays],
            in_specs=[anywhere] * (len(arrays) + 1),
            out_specs=[anywhere] * len(arrays),
            input_output_aliases={i: i for i in range(len(arrays))},
            compiler_params=params(1),
            name=name,
        )(*arrays, after)

    onward_half, return_half = pl.pallas_call(
        halves_kernel,
        out_shape=[jax.ShapeDtypeStruct((half, rows, width), f32)] * 2,
        in_specs=[anywhere] * 2,
        out_specs=[anywhere] * 2,
        scratch_shapes=[pltpu.VMEM(b.shape, f32)] + [pltpu.SemaphoreType.DMA((2 * half,))] * 2,
        compiler_params=params(8),
        cost_estimate=pl.CostEstimate(flops=0, bytes_accessed=b.size * 8, transcendentals=0),
        name="halves",
    )(before, after)
    far_0 = lax.ppermute(onward_half, "pz", onward)
    far_1 = lax.ppermute(return_half, "pz", return_)

    parts = 8
    applied = pl.pallas_call(
        functools.partial(time_kernel, weights, parts),
        out_shape=jax.ShapeDtypeStruct(sent.shape, f32),
        in_specs=[in_memory, anywhere],
        out_specs=in_memory,
        scratch_shapes=[pltpu.VMEM(sent.shape, f32)] * 2
        + [pltpu.SemaphoreType.DMA((1, parts)), pltpu.SemaphoreType.DMA((parts,))],
        compiler_params=params(60),
        cost_estimate=pl.CostEstimate(flops=sent.size * 16, bytes_accessed=sent.size * 8, transcendentals=0),
        name="time_term",
    )(sent, token)
    time_term = exchange(applied).reshape(planes, rows, width)

    with_other = lambda r: (r, lax.ppermute(r, "pz", partner))
    last_low = half // pair - 1
    in_lower, in_upper = spec(lambda s: jnp.minimum(s, last_low)), spec(lambda s: jnp.maximum(s - last_low - 1, 0))

    def line_terms(kernel, name, chips, size, specs, operands):
        return pl.pallas_call(
            kernel,
            out_shape=[jax.ShapeDtypeStruct(b.shape, f32), jax.ShapeDtypeStruct((8, width), f32)],
            grid_spec=pltpu.PrefetchScalarGridSpec(
                num_scalar_prefetch=1, grid=(planes // pair,), in_specs=specs, out_specs=[two, fixed(8, width)]
            ),
            compiler_params=params(size),
            cost_estimate=pl.CostEstimate(
                flops=12 * chips * cores * width * b.size, bytes_accessed=b.size * 4 * (3 + 2 * chips), transcendentals=0
            ),
            name=name,
        )(core, *operands)

    operands = (early, *with_other(before), *with_other(after), u, part)
    steps, token = line_terms(early_kernel, "early_terms", 2, 40, [table(early)] + [two] * 6, operands)
    far_0, far_1 = follow("follow_early", far_0, far_1, after=token)
    operands = (late, *with_other(far_0), *with_other(far_1), u, steps)
    specs = [table(late)] + [in_lower] * 2 + [in_upper] * 2 + [two] * 2
    steps, _ = line_terms(functools.partial(late_kernel, half // pair), "late_terms", 1, 40, specs, operands)

    out = pl.pallas_call(
        functools.partial(last_kernel, planes),
        out_shape=jax.ShapeDtypeStruct(b.shape, f32),
        in_specs=[pl.BlockSpec(memory_space=pltpu.VMEM)] + [in_memory] * 2,
        out_specs=in_memory,
        input_output_aliases={2: 0},
        scratch_shapes=[pltpu.VMEM(b.shape, f32)] * 3
        + [pltpu.SemaphoreType.DMA((2, planes)), pltpu.SemaphoreType.DMA((planes,))],
        compiler_params=params(60),
        cost_estimate=pl.CostEstimate(flops=2 * b.size, bytes_accessed=b.size * 16, transcendentals=0),
        name="last",
    )(inv, time_term, steps)
    return out[None]


def solution(mesh):
    spec = P("inst", "px", None, "pz")
    return jax.shard_map(on_device, mesh=mesh, in_specs=(spec,) * 5, out_specs=spec, check_vma=False)
```

```python
import functools
import math

import jax
import jax.numpy as jnp
import ml_dtypes
import numpy as np
from jax import lax
from jax.experimental import pallas as pl
from jax.experimental.pallas import tpu as pltpu
from jax.sharding import PartitionSpec as P

box_length = 4.0 * math.pi
diffusivity = 0.01
omega_tide = 4.0
coupling = 50.0
span_step = 0.05

f32 = jnp.float32
bf16 = jnp.bfloat16


def first_line(count):
    d = np.arange(count)
    sign = 1.0 - 2.0 * (d % 2)
    safe = np.where(d == 0, 1.0, np.tan(np.pi * d / count))
    return np.where(d == 0, 0.0, 0.5 * sign / safe)


def second_line(count):
    d = np.arange(count)
    sign = 1.0 - 2.0 * (d % 2)
    safe = np.where(d == 0, 1.0, np.sin(np.pi * d / count))
    return np.where(d == 0, -(count * count) / 12.0 - 1.0 / 6.0, -0.5 * sign / (safe * safe))


def wall_table(count):
    order = count - 1
    j = np.arange(count)
    angle = np.pi * j / order
    ends = (j == 0) | (j == order)
    c = np.where(ends, 2.0, 1.0) * (1.0 - 2.0 * (j % 2))
    total = j[:, None] + j[None, :]
    differ = j[:, None] - j[None, :]
    gap = -2.0 * np.sin(np.pi * total / (2 * order)) * np.sin(np.pi * differ / (2 * order))
    table = c[:, None] / c[None, :] / np.where(differ == 0, 1.0, gap)
    corner = (2.0 * order * order + 1.0) / 6.0
    sine_sq = np.where(ends, 1.0, np.sin(angle) ** 2)
    centre = -np.cos(angle) / (2.0 * sine_sq)
    centre[0], centre[order] = corner, -corner
    table = np.where(differ == 0, np.diag(centre), table)
    spacing = np.pi / order * (np.sin(angle) + np.pi / order)
    return table, spacing


def three_parts(table, axis):
    high = table.astype(np.float32).astype(ml_dtypes.bfloat16)
    low = (table - high.astype(np.float64)).astype(np.float32).astype(ml_dtypes.bfloat16)
    return np.concatenate([high, high, low], axis=axis)


def split(x):
    high = x.astype(bf16)
    return high, (x - high.astype(f32)).astype(bf16)


def derivatives(blocks, table):
    planes, rows, width = blocks[0].shape
    parts = [split(x.reshape(planes * rows, width)) for x in blocks]
    high, low = ([p[i] for p in parts] for i in range(2))
    both = jnp.dot(jnp.concatenate(high + low + high, axis=1), table, preferred_element_type=f32)
    return both[:, :width].reshape(planes, rows, width), both[:, width:].reshape(planes, rows, width)


def wall_kernel(dx, core_ref, wall_ref, line_ref, scale_ref, b_ref, edge_ref, other_ref, u_ref, v_ref, w_ref, n_ref, part_ref, inv_ref, token_ref):
    count, rows, width = b_ref.shape
    pair = u_ref.shape[0]
    start = pl.program_id(0) * pair
    here = b_ref[pl.ds(start, pair)]
    high, low = split(jnp.concatenate([here[i] for i in range(pair)], axis=1))
    both = jnp.dot(wall_ref[...], jnp.concatenate([high, low, high], axis=0), preferred_element_type=f32)
    grad_x, curv_x = derivatives([here, other_ref[...]], line_ref[0])
    for i in range(pair):
        z = start + i
        lanes = slice(i * width, (i + 1) * width)
        u, v, w = (r[i].astype(f32) for r in (u_ref, v_ref, w_ref))
        above = jnp.where(z == count - 1, edge_ref[0], b_ref[jnp.minimum(z + 1, count - 1)])
        below = jnp.where(z == 0, edge_ref[1], b_ref[jnp.maximum(z - 1, 0)])
        grad_z = (above - below) * (1.0 / (2.0 * span_step))
        curv_z = (above - 2.0 * here[i] + below) * (diffusivity / (span_step * span_step))
        radius = scale_ref[1] + jnp.abs(u) * (1.0 / dx) + jnp.abs(v) * scale_ref[0] + jnp.abs(w) * (1.0 / span_step)
        inv_ref[i] = 1.0 / radius
        advect = u * grad_x[i] + v * both[:rows, lanes] + w * grad_z
        part_ref[i] = -advect - (curv_x[i] + both[rows:, lanes] + curv_z) - coupling * n_ref[i]
    token_ref[...] = jnp.zeros_like(token_ref)


def early_kernel(core_ref, table_ref, *refs):
    blocks, (u_ref, part_ref, out_ref, token_ref) = refs[:4], refs[4:]
    grad_x, curv_x = derivatives([r[...] for r in blocks], table_ref[0])
    out_ref[...] = part_ref[...] - (u_ref[...].astype(f32) * grad_x + curv_x)
    token_ref[...] = jnp.zeros_like(token_ref)


def late_kernel(half, core_ref, table_ref, *refs):
    lower, upper = refs[:2], refs[2:4]
    u_ref, steps_ref, out_ref, token_ref = refs[4:]
    second = pl.program_id(0) >= half
    grad_x, curv_x = derivatives([jnp.where(second, y[...], x[...]) for x, y in zip(lower, upper)], table_ref[0])
    out_ref[...] = steps_ref[...] - (u_ref[...].astype(f32) * grad_x + curv_x)
    token_ref[...] = jnp.zeros_like(token_ref)


def halves_kernel(before_ref, after_ref, onward_ref, return_ref, held, in_sems, out_sems):
    half = onward_ref.shape[0]
    planes = [(before_ref.at[k], onward_ref.at[k]) for k in range(half)]
    planes += [(after_ref.at[half + k], return_ref.at[k]) for k in range(half)]
    come = [pltpu.make_async_copy(x, held.at[k], in_sems.at[k]) for k, (x, _) in enumerate(planes)]
    go = [pltpu.make_async_copy(held.at[k], y, out_sems.at[k]) for k, (_, y) in enumerate(planes)]
    for copy in come:
        copy.start()
    for first, second in zip(come, go):
        first.wait()
        second.start()
    for copy in go:
        copy.wait()


def follow_kernel(*refs):
    pass


def in_parts(count, sources, buffers, result, target, in_sems, out_sems, work):
    def part(k):
        return [pltpu.make_async_copy(x.at[at], y.at[at], in_sems.at[i, k]) for i, (x, y) in enumerate(zip(sources, buffers))]

    def out(k):
        return pltpu.make_async_copy(result.at[at], target.at[at], out_sems.at[k])

    for k in range(count):
        at = work.where(k)
        for copy in part(k):
            copy.start()
    for k in range(count):
        at = work.where(k)
        for copy in part(k):
            copy.wait()
        work.do(k)
        out(k).start()
    for k in range(count):
        at = work.where(k)
        out(k).wait()


class TimePart:
    def __init__(self, weights, size, source, result):
        self.weights, self.size, self.source, self.result = weights, size, source, result

    def where(self, k):
        return (slice(None), pl.ds(k * self.size, self.size))

    def do(self, k):
        weights, count = self.weights, self.source.shape[0]
        half = count // 2

        def body(step, carry):
            rows = pl.ds(pl.multiple_of(k * self.size + step * 8, 8), 8)
            b = [self.source[i, rows, :] for i in range(count)]
            totals = [weights[half] * b[(i + half) % count] for i in range(count)]
            for i in range(half):
                for d in range(1, half):
                    differ = b[(i + d) % count] - b[(i - d) % count]
                    totals[i] = totals[i] + weights[d] * differ
                    totals[i + half] = totals[i + half] - weights[half - d] * differ
            for i in range(count):
                self.result[i, rows, :] = totals[i]
            return carry

        lax.fori_loop(0, self.size // 8, body, 0)


class LastPart:
    def __init__(self, size, steps, time, inv, result):
        self.size, self.steps, self.time, self.inv, self.result = size, steps, time, inv, result

    def where(self, k):
        return (pl.ds(k * self.size, self.size),)

    def do(self, k):
        at = self.where(k)
        self.result[at] = (self.steps[at] - self.time[at]) * self.inv[at]


def time_kernel(weights, parts, in_ref, *refs):
    out_ref, source, result, in_sems, out_sems = refs[-5:]
    work = TimePart(weights, in_ref.shape[1] // parts, source, result)
    in_parts(parts, [in_ref], [source], result, out_ref, in_sems, out_sems, work)


def last_kernel(parts, inv_ref, time_ref, steps_ref, out_ref, time, steps, result, in_sems, out_sems):
    work = LastPart(steps_ref.shape[0] // parts, steps, time, inv_ref, result)
    in_parts(parts, [time_ref, steps_ref], [time, steps], result, out_ref, in_sems, out_sems, work)


def on_device(stream_vel, normal_vel, span_vel, adjoint_buoy, adjoint_normal):
    _, planes, rows, width = adjoint_buoy.shape
    count_x, count_i, count_p = (lax.axis_size(a) for a in ("pz", "inst", "px"))
    full = width * count_x
    dx = box_length / full
    wave = 2.0 * math.pi / box_length

    cores = 2
    groups = (0,), (-1, 1), (2,)

    def line_table(core, chips):
        offsets = [cores * step + other - core for step in chips for other in (core, 1 - core)]
        k = np.concatenate([np.arange(width) + width * o for o in offsets])
        d = (np.arange(width)[None, :] - k[:, None]) % full
        table = np.concatenate([wave * first_line(full)[d], diffusivity * wave * wave * second_line(full)[d]], axis=1)
        return three_parts(table, 0)

    first, early, late = (jnp.asarray(np.stack([line_table(c, t) for c in range(cores)])) for t in groups)
    normal_table, spacing = wall_table(rows)
    wall = np.concatenate([normal_table, diffusivity * (normal_table @ normal_table)], axis=0)
    wall = jnp.asarray(three_parts(wall, 1))
    steady = 1.0 + omega_tide * count_i / 2.0 + 2.0 * diffusivity * (1.0 / dx**2 + 1.0 / spacing**2 + 1.0 / span_step**2)
    scale = np.stack([1.0 / spacing, steady]).astype(np.float32)[:, :, None]
    scale = np.broadcast_to(scale, (2, rows, width))
    weights = [float(x) for x in omega_tide * first_line(count_i)]

    core = (lax.axis_index("pz") % cores).astype(jnp.int32).reshape(1)

    b, u, v, w, n = (x[0] for x in (adjoint_buoy, stream_vel, normal_vel, span_vel, adjoint_normal))

    share = planes * rows // count_i
    exchange = functools.partial(lax.all_to_all, axis_name="inst", split_axis=0, concat_axis=0, tiled=True)
    sent = exchange(b.reshape(count_i, share, width))

    members = range(count_x)
    onward = [(i, (i + cores) % count_x) for i in members]
    return_ = [(j, i) for i, j in onward]
    partner = [(i, i ^ 1) for i in members]
    half = planes // 2
    before = lax.ppermute(b, "pz", onward)
    after = lax.ppermute(b, "pz", return_)
    other = lax.ppermute(b, "pz", partner)
    swap = [(i, (i + 1) % count_p) for i in range(count_p)]
    back = [(j, i) for i, j in swap]
    if count_p == 2:
        edge = lax.ppermute(jnp.stack([b[0], b[planes - 1]]), "px", swap)
    else:
        edge = jnp.stack([lax.ppermute(b[0], "px", back), lax.ppermute(b[planes - 1], "px", swap)])

    pair = 2
    anywhere, in_memory = pl.BlockSpec(memory_space=pl.ANY), pl.BlockSpec(memory_space=pltpu.HBM)
    params = lambda size: pltpu.CompilerParams(vmem_limit_bytes=size * 2**20)
    spec = lambda f: pl.BlockSpec((pair, rows, width), lambda s, c: (f(s), 0, 0))
    two = spec(lambda s: s)
    fixed = lambda *shape: pl.BlockSpec(shape, lambda s, c: (0,) * len(shape))
    table = lambda t: pl.BlockSpec((1,) + t.shape[1:], lambda s, c: (c[0], 0, 0))
    part, inv, token = pl.pallas_call(
        functools.partial(wall_kernel, dx),
        out_shape=[jax.ShapeDtypeStruct(b.shape, f32)] * 2 + [jax.ShapeDtypeStruct((8, width), f32)],
        grid_spec=pltpu.PrefetchScalarGridSpec(
            num_scalar_prefetch=1,
            grid=(planes // pair,),
            in_specs=[fixed(*wall.shape), table(first), fixed(*scale.shape), fixed(*b.shape), fixed(2, rows, width)] + [two] * 5,
            out_specs=[two] * 2 + [fixed(8, width)],
        ),
        compiler_params=params(24),
        cost_estimate=pl.CostEstimate(flops=16 * rows * b.size, bytes_accessed=b.size * 28, transcendentals=0),
        name="wall_terms",
    )(core, wall, first, jnp.asarray(scale), b, edge, other, u, v, w, n)

    def follow(name, *arrays, after):
        return pl.pallas_call(
            follow_kernel,
            out_shape=[jax.ShapeDtypeStruct(x.shape, f32) for x in arrays],
            in_specs=[anywhere] * (len(arrays) + 1),
            out_specs=[anywhere] * len(arrays),
            input_output_aliases={i: i for i in range(len(arrays))},
            compiler_params=params(1),
            name=name,
        )(*arrays, after)

    onward_half, return_half = pl.pallas_call(
        halves_kernel,
        out_shape=[jax.ShapeDtypeStruct((half, rows, width), f32)] * 2,
        in_specs=[anywhere] * 2,
        out_specs=[anywhere] * 2,
        scratch_shapes=[pltpu.VMEM(b.shape, f32)] + [pltpu.SemaphoreType.DMA((2 * half,))] * 2,
        compiler_params=params(8),
        cost_estimate=pl.CostEstimate(flops=0, bytes_accessed=b.size * 8, transcendentals=0),
        name="halves",
    )(before, after)
    far_0 = lax.ppermute(onward_half, "pz", onward)
    far_1 = lax.ppermute(return_half, "pz", return_)

    parts = 8
    applied = pl.pallas_call(
        functools.partial(time_kernel, weights, parts),
        out_shape=jax.ShapeDtypeStruct(sent.shape, f32),
        in_specs=[in_memory, anywhere],
        out_specs=in_memory,
        scratch_shapes=[pltpu.VMEM(sent.shape, f32)] * 2
        + [pltpu.SemaphoreType.DMA((1, parts)), pltpu.SemaphoreType.DMA((parts,))],
        compiler_params=params(60),
        cost_estimate=pl.CostEstimate(flops=sent.size * 16, bytes_accessed=sent.size * 8, transcendentals=0),
        name="time_term",
    )(sent, token)
    time_term = exchange(applied).reshape(planes, rows, width)

    with_other = lambda r: (r, lax.ppermute(r, "pz", partner))
    last_low = half // pair - 1
    in_lower, in_upper = spec(lambda s: jnp.minimum(s, last_low)), spec(lambda s: jnp.maximum(s - last_low - 1, 0))

    def line_terms(kernel, name, chips, size, specs, operands):
        return pl.pallas_call(
            kernel,
            out_shape=[jax.ShapeDtypeStruct(b.shape, f32), jax.ShapeDtypeStruct((8, width), f32)],
            grid_spec=pltpu.PrefetchScalarGridSpec(
                num_scalar_prefetch=1, grid=(planes // pair,), in_specs=specs, out_specs=[two, fixed(8, width)]
            ),
            compiler_params=params(size),
            cost_estimate=pl.CostEstimate(
                flops=12 * chips * cores * width * b.size, bytes_accessed=b.size * 4 * (3 + 2 * chips), transcendentals=0
            ),
            name=name,
        )(core, *operands)

    operands = (early, *with_other(before), *with_other(after), u, part)
    steps, token = line_terms(early_kernel, "early_terms", 2, 40, [table(early)] + [two] * 6, operands)
    far_0, far_1 = follow("follow_early", far_0, far_1, after=token)
    operands = (late, *with_other(far_0), *with_other(far_1), u, steps)
    specs = [table(late)] + [in_lower] * 2 + [in_upper] * 2 + [two] * 2
    steps, _ = line_terms(functools.partial(late_kernel, half // pair), "late_terms", 1, 40, specs, operands)

    out = pl.pallas_call(
        functools.partial(last_kernel, planes),
        out_shape=jax.ShapeDtypeStruct(b.shape, f32),
        in_specs=[pl.BlockSpec(memory_space=pltpu.VMEM)] + [in_memory] * 2,
        out_specs=in_memory,
        input_output_aliases={2: 0},
        scratch_shapes=[pltpu.VMEM(b.shape, f32)] * 3
        + [pltpu.SemaphoreType.DMA((2, planes)), pltpu.SemaphoreType.DMA((planes,))],
        compiler_params=params(16),
        cost_estimate=pl.CostEstimate(flops=2 * b.size, bytes_accessed=b.size * 16, transcendentals=0),
        name="last",
    )(inv, time_term, steps)
    return out[None]


def solution(mesh):
    spec = P("inst", "px", None, "pz")
    return jax.shard_map(on_device, mesh=mesh, in_specs=(spec,) * 5, out_specs=spec, check_vma=False)
```

```python
import functools
import math

import jax
import jax.numpy as jnp
import ml_dtypes
import numpy as np
from jax import lax
from jax.experimental import pallas as pl
from jax.experimental.pallas import tpu as pltpu
from jax.sharding import PartitionSpec as P

box_length = 4.0 * math.pi
diffusivity = 0.01
omega_tide = 4.0
coupling = 50.0
span_step = 0.05

f32 = jnp.float32
bf16 = jnp.bfloat16


def first_line(count):
    d = np.arange(count)
    sign = 1.0 - 2.0 * (d % 2)
    safe = np.where(d == 0, 1.0, np.tan(np.pi * d / count))
    return np.where(d == 0, 0.0, 0.5 * sign / safe)


def second_line(count):
    d = np.arange(count)
    sign = 1.0 - 2.0 * (d % 2)
    safe = np.where(d == 0, 1.0, np.sin(np.pi * d / count))
    return np.where(d == 0, -(count * count) / 12.0 - 1.0 / 6.0, -0.5 * sign / (safe * safe))


def wall_table(count):
    order = count - 1
    j = np.arange(count)
    angle = np.pi * j / order
    ends = (j == 0) | (j == order)
    c = np.where(ends, 2.0, 1.0) * (1.0 - 2.0 * (j % 2))
    total = j[:, None] + j[None, :]
    differ = j[:, None] - j[None, :]
    gap = -2.0 * np.sin(np.pi * total / (2 * order)) * np.sin(np.pi * differ / (2 * order))
    table = c[:, None] / c[None, :] / np.where(differ == 0, 1.0, gap)
    corner = (2.0 * order * order + 1.0) / 6.0
    sine_sq = np.where(ends, 1.0, np.sin(angle) ** 2)
    centre = -np.cos(angle) / (2.0 * sine_sq)
    centre[0], centre[order] = corner, -corner
    table = np.where(differ == 0, np.diag(centre), table)
    spacing = np.pi / order * (np.sin(angle) + np.pi / order)
    return table, spacing


def three_parts(table, axis):
    high = table.astype(np.float32).astype(ml_dtypes.bfloat16)
    low = (table - high.astype(np.float64)).astype(np.float32).astype(ml_dtypes.bfloat16)
    return np.concatenate([high, high, low], axis=axis)


def split(x):
    high = x.astype(bf16)
    return high, (x - high.astype(f32)).astype(bf16)


def derivatives(blocks, table):
    planes, rows, width = blocks[0].shape
    parts = [split(x.reshape(planes * rows, width)) for x in blocks]
    high, low = ([p[i] for p in parts] for i in range(2))
    both = jnp.dot(jnp.concatenate(high + low + high, axis=1), table, preferred_element_type=f32)
    return both[:, :width].reshape(planes, rows, width), both[:, width:].reshape(planes, rows, width)


def wall_kernel(dx, core_ref, wall_ref, line_ref, scale_ref, b_ref, edge_ref, other_ref, u_ref, v_ref, w_ref, n_ref, part_ref, inv_ref, token_ref):
    count, rows, width = b_ref.shape
    pair = u_ref.shape[0]
    start = pl.program_id(0) * pair
    here = b_ref[pl.ds(start, pair)]
    high, low = split(jnp.concatenate([here[i] for i in range(pair)], axis=1))
    both = jnp.dot(wall_ref[...], jnp.concatenate([high, low, high], axis=0), preferred_element_type=f32)
    grad_x, curv_x = derivatives([here, other_ref[...]], line_ref[0])
    for i in range(pair):
        z = start + i
        lanes = slice(i * width, (i + 1) * width)
        u, v, w = (r[i].astype(f32) for r in (u_ref, v_ref, w_ref))
        above = jnp.where(z == count - 1, edge_ref[0], b_ref[jnp.minimum(z + 1, count - 1)])
        below = jnp.where(z == 0, edge_ref[1], b_ref[jnp.maximum(z - 1, 0)])
        grad_z = (above - below) * (1.0 / (2.0 * span_step))
        curv_z = (above - 2.0 * here[i] + below) * (diffusivity / (span_step * span_step))
        radius = scale_ref[1] + jnp.abs(u) * (1.0 / dx) + jnp.abs(v) * scale_ref[0] + jnp.abs(w) * (1.0 / span_step)
        inv_ref[i] = 1.0 / radius
        advect = u * grad_x[i] + v * both[:rows, lanes] + w * grad_z
        part_ref[i] = -advect - (curv_x[i] + both[rows:, lanes] + curv_z) - coupling * n_ref[i]
    token_ref[...] = jnp.zeros_like(token_ref)


def early_kernel(core_ref, table_ref, *refs):
    blocks, (u_ref, part_ref, out_ref, token_ref) = refs[:4], refs[4:]
    grad_x, curv_x = derivatives([r[...] for r in blocks], table_ref[0])
    out_ref[...] = part_ref[...] - (u_ref[...].astype(f32) * grad_x + curv_x)
    token_ref[...] = jnp.zeros_like(token_ref)


def late_kernel(half, core_ref, table_ref, *refs):
    lower, upper = refs[:2], refs[2:4]
    u_ref, steps_ref, out_ref, token_ref = refs[4:]
    second = pl.program_id(0) >= half
    grad_x, curv_x = derivatives([jnp.where(second, y[...], x[...]) for x, y in zip(lower, upper)], table_ref[0])
    out_ref[...] = steps_ref[...] - (u_ref[...].astype(f32) * grad_x + curv_x)
    token_ref[...] = jnp.zeros_like(token_ref)


def halves_kernel(before_ref, after_ref, onward_ref, return_ref, held, in_sems, out_sems):
    half = onward_ref.shape[0]
    planes = [(before_ref.at[k], onward_ref.at[k]) for k in range(half)]
    planes += [(after_ref.at[half + k], return_ref.at[k]) for k in range(half)]
    come = [pltpu.make_async_copy(x, held.at[k], in_sems.at[k]) for k, (x, _) in enumerate(planes)]
    go = [pltpu.make_async_copy(held.at[k], y, out_sems.at[k]) for k, (_, y) in enumerate(planes)]
    for copy in come:
        copy.start()
    for first, second in zip(come, go):
        first.wait()
        second.start()
    for copy in go:
        copy.wait()


def follow_kernel(*refs):
    pass


def in_parts(count, sources, buffers, result, target, in_sems, out_sems, work):
    def part(k):
        return [pltpu.make_async_copy(x.at[at], y.at[at], in_sems.at[i, k]) for i, (x, y) in enumerate(zip(sources, buffers))]

    def out(k):
        return pltpu.make_async_copy(result.at[at], target.at[at], out_sems.at[k])

    for k in range(count):
        at = work.where(k)
        for copy in part(k):
            copy.start()
    for k in range(count):
        at = work.where(k)
        for copy in part(k):
            copy.wait()
        work.do(k)
        out(k).start()
    for k in range(count):
        at = work.where(k)
        out(k).wait()


class TimePart:
    def __init__(self, weights, size, source, result):
        self.weights, self.size, self.source, self.result = weights, size, source, result

    def where(self, k):
        return (slice(None), pl.ds(k * self.size, self.size))

    def do(self, k):
        weights, count = self.weights, self.source.shape[0]
        half = count // 2

        def body(step, carry):
            rows = pl.ds(pl.multiple_of(k * self.size + step * 8, 8), 8)
            b = [self.source[i, rows, :] for i in range(count)]
            totals = [weights[half] * b[(i + half) % count] for i in range(count)]
            for i in range(half):
                for d in range(1, half):
                    differ = b[(i + d) % count] - b[(i - d) % count]
                    totals[i] = totals[i] + weights[d] * differ
                    totals[i + half] = totals[i + half] - weights[half - d] * differ
            for i in range(count):
                self.result[i, rows, :] = totals[i]
            return carry

        lax.fori_loop(0, self.size // 8, body, 0)


class LastPart:
    def __init__(self, size, steps, time, inv, result):
        self.size, self.steps, self.time, self.inv, self.result = size, steps, time, inv, result

    def where(self, k):
        return (pl.ds(k * self.size, self.size),)

    def do(self, k):
        at = self.where(k)
        self.result[at] = (self.steps[at] - self.time[at]) * self.inv[at]


def time_kernel(weights, parts, in_ref, *refs):
    out_ref, source, result, in_sems, out_sems = refs[-5:]
    work = TimePart(weights, in_ref.shape[1] // parts, source, result)
    in_parts(parts, [in_ref], [source], result, out_ref, in_sems, out_sems, work)


def last_kernel(parts, inv_ref, time_ref, steps_ref, out_ref, time, steps, result, in_sems, out_sems):
    work = LastPart(steps_ref.shape[0] // parts, steps, time, inv_ref, result)
    in_parts(parts, [time_ref, steps_ref], [time, steps], result, out_ref, in_sems, out_sems, work)


def on_device(stream_vel, normal_vel, span_vel, adjoint_buoy, adjoint_normal):
    _, planes, rows, width = adjoint_buoy.shape
    count_x, count_i, count_p = (lax.axis_size(a) for a in ("pz", "inst", "px"))
    full = width * count_x
    dx = box_length / full
    wave = 2.0 * math.pi / box_length

    cores = 2
    groups = (0,), (-1, 1), (2,)

    def line_table(core, chips):
        offsets = [cores * step + other - core for step in chips for other in (core, 1 - core)]
        k = np.concatenate([np.arange(width) + width * o for o in offsets])
        d = (np.arange(width)[None, :] - k[:, None]) % full
        table = np.concatenate([wave * first_line(full)[d], diffusivity * wave * wave * second_line(full)[d]], axis=1)
        return three_parts(table, 0)

    first, early, late = (jnp.asarray(np.stack([line_table(c, t) for c in range(cores)])) for t in groups)
    normal_table, spacing = wall_table(rows)
    wall = np.concatenate([normal_table, diffusivity * (normal_table @ normal_table)], axis=0)
    wall = jnp.asarray(three_parts(wall, 1))
    steady = 1.0 + omega_tide * count_i / 2.0 + 2.0 * diffusivity * (1.0 / dx**2 + 1.0 / spacing**2 + 1.0 / span_step**2)
    scale = np.stack([1.0 / spacing, steady]).astype(np.float32)[:, :, None]
    scale = np.broadcast_to(scale, (2, rows, width))
    weights = [float(x) for x in omega_tide * first_line(count_i)]

    core = (lax.axis_index("pz") % cores).astype(jnp.int32).reshape(1)

    b, u, v, w, n = (x[0] for x in (adjoint_buoy, stream_vel, normal_vel, span_vel, adjoint_normal))

    share = planes * rows // count_i
    exchange = functools.partial(lax.all_to_all, axis_name="inst", split_axis=0, concat_axis=0, tiled=True)
    sent = exchange(b.reshape(count_i, share, width))

    members = range(count_x)
    onward = [(i, (i + cores) % count_x) for i in members]
    return_ = [(j, i) for i, j in onward]
    partner = [(i, i ^ 1) for i in members]
    half = planes // 2
    before = lax.ppermute(b, "pz", onward)
    after = lax.ppermute(b, "pz", return_)
    other = lax.ppermute(b, "pz", partner)
    swap = [(i, (i + 1) % count_p) for i in range(count_p)]
    back = [(j, i) for i, j in swap]
    if count_p == 2:
        edge = lax.ppermute(jnp.stack([b[0], b[planes - 1]]), "px", swap)
    else:
        edge = jnp.stack([lax.ppermute(b[0], "px", back), lax.ppermute(b[planes - 1], "px", swap)])

    pair = 2
    anywhere, in_memory = pl.BlockSpec(memory_space=pl.ANY), pl.BlockSpec(memory_space=pltpu.HBM)
    params = lambda size: pltpu.CompilerParams(vmem_limit_bytes=size * 2**20)
    spec = lambda f: pl.BlockSpec((pair, rows, width), lambda s, c: (f(s), 0, 0))
    two = spec(lambda s: s)
    fixed = lambda *shape: pl.BlockSpec(shape, lambda s, c: (0,) * len(shape))
    table = lambda t: pl.BlockSpec((1,) + t.shape[1:], lambda s, c: (c[0], 0, 0))
    part, inv, token = pl.pallas_call(
        functools.partial(wall_kernel, dx),
        out_shape=[jax.ShapeDtypeStruct(b.shape, f32)] * 2 + [jax.ShapeDtypeStruct((8, width), f32)],
        grid_spec=pltpu.PrefetchScalarGridSpec(
            num_scalar_prefetch=1,
            grid=(planes // pair,),
            in_specs=[fixed(*wall.shape), table(first), fixed(*scale.shape), fixed(*b.shape), fixed(2, rows, width)] + [two] * 5,
            out_specs=[two] * 2 + [fixed(8, width)],
        ),
        compiler_params=params(24),
        cost_estimate=pl.CostEstimate(flops=16 * rows * b.size, bytes_accessed=b.size * 28, transcendentals=0),
        name="wall_terms",
    )(core, wall, first, jnp.asarray(scale), b, edge, other, u, v, w, n)

    def follow(name, *arrays, after):
        return pl.pallas_call(
            follow_kernel,
            out_shape=[jax.ShapeDtypeStruct(x.shape, f32) for x in arrays],
            in_specs=[anywhere] * (len(arrays) + 1),
            out_specs=[anywhere] * len(arrays),
            input_output_aliases={i: i for i in range(len(arrays))},
            compiler_params=params(1),
            name=name,
        )(*arrays, after)

    onward_half, return_half = pl.pallas_call(
        halves_kernel,
        out_shape=[jax.ShapeDtypeStruct((half, rows, width), f32)] * 2,
        in_specs=[anywhere] * 2,
        out_specs=[anywhere] * 2,
        scratch_shapes=[pltpu.VMEM(b.shape, f32)] + [pltpu.SemaphoreType.DMA((2 * half,))] * 2,
        compiler_params=params(8),
        cost_estimate=pl.CostEstimate(flops=0, bytes_accessed=b.size * 8, transcendentals=0),
        name="halves",
    )(before, after)
    far_0 = lax.ppermute(onward_half, "pz", onward)
    far_1 = lax.ppermute(return_half, "pz", return_)

    parts = 8
    applied = pl.pallas_call(
        functools.partial(time_kernel, weights, parts),
        out_shape=jax.ShapeDtypeStruct(sent.shape, f32),
        in_specs=[in_memory, anywhere],
        out_specs=in_memory,
        scratch_shapes=[pltpu.VMEM(sent.shape, f32)] * 2
        + [pltpu.SemaphoreType.DMA((1, parts)), pltpu.SemaphoreType.DMA((parts,))],
        compiler_params=params(16),
        cost_estimate=pl.CostEstimate(flops=sent.size * 16, bytes_accessed=sent.size * 8, transcendentals=0),
        name="time_term",
    )(sent, token)
    time_term = exchange(applied).reshape(planes, rows, width)

    with_other = lambda r: (r, lax.ppermute(r, "pz", partner))
    last_low = half // pair - 1
    in_lower, in_upper = spec(lambda s: jnp.minimum(s, last_low)), spec(lambda s: jnp.maximum(s - last_low - 1, 0))

    def line_terms(kernel, name, chips, size, specs, operands):
        return pl.pallas_call(
            kernel,
            out_shape=[jax.ShapeDtypeStruct(b.shape, f32), jax.ShapeDtypeStruct((8, width), f32)],
            grid_spec=pltpu.PrefetchScalarGridSpec(
                num_scalar_prefetch=1, grid=(planes // pair,), in_specs=specs, out_specs=[two, fixed(8, width)]
            ),
            compiler_params=params(size),
            cost_estimate=pl.CostEstimate(
                flops=12 * chips * cores * width * b.size, bytes_accessed=b.size * 4 * (3 + 2 * chips), transcendentals=0
            ),
            name=name,
        )(core, *operands)

    operands = (early, *with_other(before), *with_other(after), u, part)
    steps, token = line_terms(early_kernel, "early_terms", 2, 40, [table(early)] + [two] * 6, operands)
    far_0, far_1 = follow("follow_early", far_0, far_1, after=token)
    operands = (late, *with_other(far_0), *with_other(far_1), u, steps)
    specs = [table(late)] + [in_lower] * 2 + [in_upper] * 2 + [two] * 2
    steps, _ = line_terms(functools.partial(late_kernel, half // pair), "late_terms", 1, 40, specs, operands)

    out = pl.pallas_call(
        functools.partial(last_kernel, planes),
        out_shape=jax.ShapeDtypeStruct(b.shape, f32),
        in_specs=[pl.BlockSpec(memory_space=pltpu.VMEM)] + [in_memory] * 2,
        out_specs=in_memory,
        input_output_aliases={2: 0},
        scratch_shapes=[pltpu.VMEM(b.shape, f32)] * 3
        + [pltpu.SemaphoreType.DMA((2, planes)), pltpu.SemaphoreType.DMA((planes,))],
        compiler_params=params(16),
        cost_estimate=pl.CostEstimate(flops=2 * b.size, bytes_accessed=b.size * 16, transcendentals=0),
        name="last",
    )(inv, time_term, steps)
    return out[None]


def solution(mesh):
    spec = P("inst", "px", None, "pz")
    return jax.shard_map(on_device, mesh=mesh, in_specs=(spec,) * 5, out_specs=spec, check_vma=False)
```

```python
import functools
import math

import jax
import jax.numpy as jnp
import ml_dtypes
import numpy as np
from jax import lax
from jax.experimental import pallas as pl
from jax.experimental.pallas import tpu as pltpu
from jax.sharding import PartitionSpec as P

box_length = 4.0 * math.pi
diffusivity = 0.01
omega_tide = 4.0
coupling = 50.0
span_step = 0.05

f32 = jnp.float32
bf16 = jnp.bfloat16


def first_line(count):
    d = np.arange(count)
    sign = 1.0 - 2.0 * (d % 2)
    safe = np.where(d == 0, 1.0, np.tan(np.pi * d / count))
    return np.where(d == 0, 0.0, 0.5 * sign / safe)


def second_line(count):
    d = np.arange(count)
    sign = 1.0 - 2.0 * (d % 2)
    safe = np.where(d == 0, 1.0, np.sin(np.pi * d / count))
    return np.where(d == 0, -(count * count) / 12.0 - 1.0 / 6.0, -0.5 * sign / (safe * safe))


def wall_table(count):
    order = count - 1
    j = np.arange(count)
    angle = np.pi * j / order
    ends = (j == 0) | (j == order)
    c = np.where(ends, 2.0, 1.0) * (1.0 - 2.0 * (j % 2))
    total = j[:, None] + j[None, :]
    differ = j[:, None] - j[None, :]
    gap = -2.0 * np.sin(np.pi * total / (2 * order)) * np.sin(np.pi * differ / (2 * order))
    table = c[:, None] / c[None, :] / np.where(differ == 0, 1.0, gap)
    corner = (2.0 * order * order + 1.0) / 6.0
    sine_sq = np.where(ends, 1.0, np.sin(angle) ** 2)
    centre = -np.cos(angle) / (2.0 * sine_sq)
    centre[0], centre[order] = corner, -corner
    table = np.where(differ == 0, np.diag(centre), table)
    spacing = np.pi / order * (np.sin(angle) + np.pi / order)
    return table, spacing


def three_parts(table, axis):
    high = table.astype(np.float32).astype(ml_dtypes.bfloat16)
    low = (table - high.astype(np.float64)).astype(np.float32).astype(ml_dtypes.bfloat16)
    return np.concatenate([high, high, low], axis=axis)


def split(x):
    high = x.astype(bf16)
    return high, (x - high.astype(f32)).astype(bf16)


def derivatives(blocks, table):
    planes, rows, width = blocks[0].shape
    parts = [split(x.reshape(planes * rows, width)) for x in blocks]
    high, low = ([p[i] for p in parts] for i in range(2))
    both = jnp.dot(jnp.concatenate(high + low + high, axis=1), table, preferred_element_type=f32)
    return both[:, :width].reshape(planes, rows, width), both[:, width:].reshape(planes, rows, width)


def wall_kernel(dx, core_ref, wall_ref, line_ref, scale_ref, b_ref, edge_ref, other_ref, u_ref, v_ref, w_ref, n_ref, part_ref, inv_ref, token_ref):
    count, rows, width = b_ref.shape
    pair = u_ref.shape[0]
    start = pl.program_id(0) * pair
    here = b_ref[pl.ds(start, pair)]
    high, low = split(jnp.concatenate([here[i] for i in range(pair)], axis=1))
    both = jnp.dot(wall_ref[...], jnp.concatenate([high, low, high], axis=0), preferred_element_type=f32)
    grad_x, curv_x = derivatives([here, other_ref[...]], line_ref[0])
    for i in range(pair):
        z = start + i
        lanes = slice(i * width, (i + 1) * width)
        u, v, w = (r[i].astype(f32) for r in (u_ref, v_ref, w_ref))
        above = jnp.where(z == count - 1, edge_ref[0], b_ref[jnp.minimum(z + 1, count - 1)])
        below = jnp.where(z == 0, edge_ref[1], b_ref[jnp.maximum(z - 1, 0)])
        grad_z = (above - below) * (1.0 / (2.0 * span_step))
        curv_z = (above - 2.0 * here[i] + below) * (diffusivity / (span_step * span_step))
        radius = scale_ref[1] + jnp.abs(u) * (1.0 / dx) + jnp.abs(v) * scale_ref[0] + jnp.abs(w) * (1.0 / span_step)
        inv_ref[i] = 1.0 / radius
        advect = u * grad_x[i] + v * both[:rows, lanes] + w * grad_z
        part_ref[i] = -advect - (curv_x[i] + both[rows:, lanes] + curv_z) - coupling * n_ref[i]
    token_ref[...] = jnp.zeros_like(token_ref)


def early_kernel(core_ref, table_ref, *refs):
    blocks, (u_ref, part_ref, out_ref, token_ref) = refs[:4], refs[4:]
    grad_x, curv_x = derivatives([r[...] for r in blocks], table_ref[0])
    out_ref[...] = part_ref[...] - (u_ref[...].astype(f32) * grad_x + curv_x)
    token_ref[...] = jnp.zeros_like(token_ref)


def late_kernel(half, core_ref, table_ref, *refs):
    lower, upper = refs[:2], refs[2:4]
    u_ref, steps_ref, out_ref, token_ref = refs[4:]
    second = pl.program_id(0) >= half
    grad_x, curv_x = derivatives([jnp.where(second, y[...], x[...]) for x, y in zip(lower, upper)], table_ref[0])
    out_ref[...] = steps_ref[...] - (u_ref[...].astype(f32) * grad_x + curv_x)
    token_ref[...] = jnp.zeros_like(token_ref)


def halves_kernel(before_ref, after_ref, onward_ref, return_ref, held, in_sems, out_sems):
    half = onward_ref.shape[0]
    planes = [(before_ref.at[k], onward_ref.at[k]) for k in range(half)]
    planes += [(after_ref.at[half + k], return_ref.at[k]) for k in range(half)]
    come = [pltpu.make_async_copy(x, held.at[k], in_sems.at[k]) for k, (x, _) in enumerate(planes)]
    go = [pltpu.make_async_copy(held.at[k], y, out_sems.at[k]) for k, (_, y) in enumerate(planes)]
    for copy in come:
        copy.start()
    for first, second in zip(come, go):
        first.wait()
        second.start()
    for copy in go:
        copy.wait()


def follow_kernel(*refs):
    pass


def in_parts(count, sources, buffers, result, target, in_sems, out_sems, work):
    def part(k):
        return [pltpu.make_async_copy(x.at[at], y.at[at], in_sems.at[i, k]) for i, (x, y) in enumerate(zip(sources, buffers))]

    def out(k):
        return pltpu.make_async_copy(result.at[at], target.at[at], out_sems.at[k])

    for k in range(count):
        at = work.where(k)
        for copy in part(k):
            copy.start()
    for k in range(count):
        at = work.where(k)
        for copy in part(k):
            copy.wait()
        work.do(k)
        out(k).start()
    for k in range(count):
        at = work.where(k)
        out(k).wait()


class TimePart:
    def __init__(self, weights, order, size, source, result):
        self.weights, self.order, self.size, self.source, self.result = weights, order, size, source, result

    def where(self, k):
        return (slice(None), pl.ds(k * self.size, self.size))

    def do(self, k):
        weights, count = self.weights, self.source.shape[0]
        half = count // 2

        def body(step, carry):
            rows = pl.ds(pl.multiple_of(k * self.size + step * 8, 8), 8)
            b = [self.source[self.order.index(i), rows, :] for i in range(count)]
            totals = [weights[half] * b[(i + half) % count] for i in range(count)]
            for i in range(half):
                for d in range(1, half):
                    differ = b[(i + d) % count] - b[(i - d) % count]
                    totals[i] = totals[i] + weights[d] * differ
                    totals[i + half] = totals[i + half] - weights[half - d] * differ
            for i in range(count):
                self.result[self.order.index(i), rows, :] = totals[i]
            return carry

        lax.fori_loop(0, self.size // 8, body, 0)


class LastPart:
    def __init__(self, size, steps, time, inv, result):
        self.size, self.steps, self.time, self.inv, self.result = size, steps, time, inv, result

    def where(self, k):
        return (pl.ds(k * self.size, self.size),)

    def do(self, k):
        at = self.where(k)
        self.result[at] = (self.steps[at] - self.time[at]) * self.inv[at]


def time_kernel(weights, order, parts, in_ref, *refs):
    out_ref, source, result, in_sems, out_sems = refs[-5:]
    work = TimePart(weights, order, in_ref.shape[1] // parts, source, result)
    in_parts(parts, [in_ref], [source], result, out_ref, in_sems, out_sems, work)


def last_kernel(parts, inv_ref, time_ref, steps_ref, out_ref, time, steps, result, in_sems, out_sems):
    work = LastPart(steps_ref.shape[0] // parts, steps, time, inv_ref, result)
    in_parts(parts, [time_ref, steps_ref], [time, steps], result, out_ref, in_sems, out_sems, work)


def on_device(stream_vel, normal_vel, span_vel, adjoint_buoy, adjoint_normal):
    _, planes, rows, width = adjoint_buoy.shape
    count_x, count_i, count_p = (lax.axis_size(a) for a in ("pz", "inst", "px"))
    full = width * count_x
    dx = box_length / full
    wave = 2.0 * math.pi / box_length

    cores = 2
    groups = (0,), (-1, 1), (2,)

    def line_table(core, chips):
        offsets = [cores * step + other - core for step in chips for other in (core, 1 - core)]
        k = np.concatenate([np.arange(width) + width * o for o in offsets])
        d = (np.arange(width)[None, :] - k[:, None]) % full
        table = np.concatenate([wave * first_line(full)[d], diffusivity * wave * wave * second_line(full)[d]], axis=1)
        return three_parts(table, 0)

    first, early, late = (jnp.asarray(np.stack([line_table(c, t) for c in range(cores)])) for t in groups)
    normal_table, spacing = wall_table(rows)
    wall = np.concatenate([normal_table, diffusivity * (normal_table @ normal_table)], axis=0)
    wall = jnp.asarray(three_parts(wall, 1))
    steady = 1.0 + omega_tide * count_i / 2.0 + 2.0 * diffusivity * (1.0 / dx**2 + 1.0 / spacing**2 + 1.0 / span_step**2)
    scale = np.stack([1.0 / spacing, steady]).astype(np.float32)[:, :, None]
    scale = np.broadcast_to(scale, (2, rows, width))
    weights = [float(x) for x in omega_tide * first_line(count_i)]

    core = (lax.axis_index("pz") % cores).astype(jnp.int32).reshape(1)

    b, u, v, w, n = (x[0] for x in (adjoint_buoy, stream_vel, normal_vel, span_vel, adjoint_normal))

    share = planes * rows // count_i
    order = [i for i in reversed(range(count_i))]
    exchange = functools.partial(
        lax.all_to_all, axis_name="inst", split_axis=0, concat_axis=0, axis_index_groups=[order], tiled=True
    )
    sent = exchange(b.reshape(count_i, share, width))

    members = range(count_x)
    onward = [(i, (i + cores) % count_x) for i in members]
    return_ = [(j, i) for i, j in onward]
    partner = [(i, i ^ 1) for i in members]
    half = planes // 2
    before = lax.ppermute(b, "pz", onward)
    after = lax.ppermute(b, "pz", return_)
    other = lax.ppermute(b, "pz", partner)
    swap = [(i, (i + 1) % count_p) for i in range(count_p)]
    back = [(j, i) for i, j in swap]
    if count_p == 2:
        edge = lax.ppermute(jnp.stack([b[0], b[planes - 1]]), "px", swap)
    else:
        edge = jnp.stack([lax.ppermute(b[0], "px", back), lax.ppermute(b[planes - 1], "px", swap)])

    pair = 2
    anywhere, in_memory = pl.BlockSpec(memory_space=pl.ANY), pl.BlockSpec(memory_space=pltpu.HBM)
    params = lambda size: pltpu.CompilerParams(vmem_limit_bytes=size * 2**20)
    spec = lambda f: pl.BlockSpec((pair, rows, width), lambda s, c: (f(s), 0, 0))
    two = spec(lambda s: s)
    fixed = lambda *shape: pl.BlockSpec(shape, lambda s, c: (0,) * len(shape))
    table = lambda t: pl.BlockSpec((1,) + t.shape[1:], lambda s, c: (c[0], 0, 0))
    part, inv, token = pl.pallas_call(
        functools.partial(wall_kernel, dx),
        out_shape=[jax.ShapeDtypeStruct(b.shape, f32)] * 2 + [jax.ShapeDtypeStruct((8, width), f32)],
        grid_spec=pltpu.PrefetchScalarGridSpec(
            num_scalar_prefetch=1,
            grid=(planes // pair,),
            in_specs=[fixed(*wall.shape), table(first), fixed(*scale.shape), fixed(*b.shape), fixed(2, rows, width)] + [two] * 5,
            out_specs=[two] * 2 + [fixed(8, width)],
        ),
        compiler_params=params(24),
        cost_estimate=pl.CostEstimate(flops=16 * rows * b.size, bytes_accessed=b.size * 28, transcendentals=0),
        name="wall_terms",
    )(core, wall, first, jnp.asarray(scale), b, edge, other, u, v, w, n)

    def follow(name, *arrays, after):
        return pl.pallas_call(
            follow_kernel,
            out_shape=[jax.ShapeDtypeStruct(x.shape, f32) for x in arrays],
            in_specs=[anywhere] * (len(arrays) + 1),
            out_specs=[anywhere] * len(arrays),
            input_output_aliases={i: i for i in range(len(arrays))},
            compiler_params=params(1),
            name=name,
        )(*arrays, after)

    onward_half, return_half = pl.pallas_call(
        halves_kernel,
        out_shape=[jax.ShapeDtypeStruct((half, rows, width), f32)] * 2,
        in_specs=[anywhere] * 2,
        out_specs=[anywhere] * 2,
        scratch_shapes=[pltpu.VMEM(b.shape, f32)] + [pltpu.SemaphoreType.DMA((2 * half,))] * 2,
        compiler_params=params(8),
        cost_estimate=pl.CostEstimate(flops=0, bytes_accessed=b.size * 8, transcendentals=0),
        name="halves",
    )(before, after)
    far_0 = lax.ppermute(onward_half, "pz", onward)
    far_1 = lax.ppermute(return_half, "pz", return_)

    parts = 8
    applied = pl.pallas_call(
        functools.partial(time_kernel, weights, order, parts),
        out_shape=jax.ShapeDtypeStruct(sent.shape, f32),
        in_specs=[in_memory, anywhere],
        out_specs=in_memory,
        scratch_shapes=[pltpu.VMEM(sent.shape, f32)] * 2
        + [pltpu.SemaphoreType.DMA((1, parts)), pltpu.SemaphoreType.DMA((parts,))],
        compiler_params=params(60),
        cost_estimate=pl.CostEstimate(flops=sent.size * 16, bytes_accessed=sent.size * 8, transcendentals=0),
        name="time_term",
    )(sent, token)
    time_term = exchange(applied).reshape(planes, rows, width)

    with_other = lambda r: (r, lax.ppermute(r, "pz", partner))
    last_low = half // pair - 1
    in_lower, in_upper = spec(lambda s: jnp.minimum(s, last_low)), spec(lambda s: jnp.maximum(s - last_low - 1, 0))

    def line_terms(kernel, name, chips, size, specs, operands):
        return pl.pallas_call(
            kernel,
            out_shape=[jax.ShapeDtypeStruct(b.shape, f32), jax.ShapeDtypeStruct((8, width), f32)],
            grid_spec=pltpu.PrefetchScalarGridSpec(
                num_scalar_prefetch=1, grid=(planes // pair,), in_specs=specs, out_specs=[two, fixed(8, width)]
            ),
            compiler_params=params(size),
            cost_estimate=pl.CostEstimate(
                flops=12 * chips * cores * width * b.size, bytes_accessed=b.size * 4 * (3 + 2 * chips), transcendentals=0
            ),
            name=name,
        )(core, *operands)

    operands = (early, *with_other(before), *with_other(after), u, part)
    steps, token = line_terms(early_kernel, "early_terms", 2, 40, [table(early)] + [two] * 6, operands)
    far_0, far_1 = follow("follow_early", far_0, far_1, after=token)
    operands = (late, *with_other(far_0), *with_other(far_1), u, steps)
    specs = [table(late)] + [in_lower] * 2 + [in_upper] * 2 + [two] * 2
    steps, _ = line_terms(functools.partial(late_kernel, half // pair), "late_terms", 1, 40, specs, operands)

    out = pl.pallas_call(
        functools.partial(last_kernel, planes),
        out_shape=jax.ShapeDtypeStruct(b.shape, f32),
        in_specs=[pl.BlockSpec(memory_space=pltpu.VMEM)] + [in_memory] * 2,
        out_specs=in_memory,
        input_output_aliases={2: 0},
        scratch_shapes=[pltpu.VMEM(b.shape, f32)] * 3
        + [pltpu.SemaphoreType.DMA((2, planes)), pltpu.SemaphoreType.DMA((planes,))],
        compiler_params=params(16),
        cost_estimate=pl.CostEstimate(flops=2 * b.size, bytes_accessed=b.size * 16, transcendentals=0),
        name="last",
    )(inv, time_term, steps)
    return out[None]


def solution(mesh):
    spec = P("inst", "px", None, "pz")
    return jax.shard_map(on_device, mesh=mesh, in_specs=(spec,) * 5, out_specs=spec, check_vma=False)
```
